32 devices in a mesh: groups: 2 (over y), seq: 8 (over z, x), head: 2 (over core).
Axes of the slice: x: 2, y: 2, z: 4, core: 2. Of those that a mesh axis runs over, the one named last changes fastest.
Arguments:
- queries: bfloat16 [8192, 8192], P(('groups', 'seq'), 'head'), parts along dimension 0, may hold values from -32 to 32
- keys: bfloat16 [8192, 1024], P(('groups', 'seq'), 'head'), parts along dimension 0, may hold values from -32 to 32
- values: bfloat16 [8192, 1024], P(('groups', 'seq'), 'head'), parts along dimension 0, may hold values from -6 to 6
- block_lists: int32 [8, 128, 20], P('head', 'groups'), parts along dimension 1, may hold values from -1 to 63, as said below
- dec_queries: bfloat16 [512, 2, 8192], P(('groups', 'seq'), None, 'head'), parts along dimension 0, may hold values from -40 to 40
- dec_keys: bfloat16 [512, 2, 1024], P(('groups', 'seq'), None, 'head'), parts along dimension 0, may hold values from -40 to 40
- decode_value_rows: bfloat16 [512, 2, 1024], P(('groups', 'seq'), None, 'head'), parts along dimension 0, may hold values from -6 to 6
- positions: int32 [512], P('groups'), parts along dimension 0, may hold values from 2048 to 4096
Outputs:
- prompt_out: bfloat16 [8192, 8192], P(('groups', 'seq'), 'head'), parts along dimension 0
- decode_out: bfloat16 [512, 2, 8192], P(('groups', 'seq'), None, 'head'), parts along dimension 0
The draws below stay inside these ranges and needn't reach their ends.
There are 2 independent parts, one for each index of `groups`. The reference program is written for one: setup_inputs(seed, part) draws one part's arguments, and reference() takes and returns one part's arrays. A program takes and returns all parts, laid end to end along the dimension named above; each array names one. Nothing has to cross between parts.
Inputs may be any that keep to these rules, and one draw needn't show every extreme that they name: In each row block_lists[h, b] the entries are distinct, entries -1 stand after all others, the first entry is b, and every entry is at most b. For each h the entries smaller than their row's b - 3 take exactly 16 distinct values.
All inputs are finite; a program needn't handle non-finite values.
Results may differ from the reference program's by a relative error of at most 0.0041.
Values may be sent and summed in bfloat16 or wider, within the bound.
No kernel may reach another device: no remote copies, remote signals or barrier semaphores. Data moves between devices by JAX's collectives and lax.ppermute only.
A program may use at most 192 MiB of HBM per device.

```python
import math
import jax
import jax.numpy as jnp
from jax import lax

QUERY_HEADS = 64
KEY_VALUE_HEADS = 8
HEAD_SIZE = 128
BLOCK_POSITIONS = 64
SLASH = 3
VERT = 16
ROLLOUT_COUNT = 256
DECODE_STEPS = 2
PROMPT_LENGTH = 4096
PROMPT_BLOCKS = 64


def prompt_common(key):
    base_offset = jax.random.fold_in(key, 101)
    leading_key = jax.random.fold_in(base_offset, 0)
    shared_prefix = jax.random.truncated_normal(leading_key, -6.0, 6.0, (PROMPT_LENGTH, KEY_VALUE_HEADS, HEAD_SIZE), jnp.float32)
    return shared_prefix


def decode_common(key):
    base_offset = jax.random.fold_in(key, 202)
    return jax.random.truncated_normal(base_offset, -6.0, 6.0, (ROLLOUT_COUNT, DECODE_STEPS, KEY_VALUE_HEADS, HEAD_SIZE), jnp.float32)


def draw_queries(key, part):
    key = jax.random.fold_in(key, 2)
    final_output = jax.random.truncated_normal(key, -6.0, 6.0, (PROMPT_LENGTH, KEY_VALUE_HEADS, QUERY_HEADS // KEY_VALUE_HEADS, HEAD_SIZE), jnp.float32)
    return final_output.reshape(PROMPT_LENGTH, QUERY_HEADS * HEAD_SIZE).astype(jnp.bfloat16)


def draw_keys(key, part):
    shared_prefix = prompt_common(key)
    final_output = shared_prefix
    return final_output.reshape(PROMPT_LENGTH, KEY_VALUE_HEADS * HEAD_SIZE).astype(jnp.bfloat16)


def draw_dec_queries(key, part):
    shared_prefix = decode_common(key)
    key = jax.random.fold_in(key, 3)
    random_noise = jax.random.truncated_normal(key, -6.0, 6.0, (ROLLOUT_COUNT, DECODE_STEPS, KEY_VALUE_HEADS, QUERY_HEADS // KEY_VALUE_HEADS, HEAD_SIZE), jnp.float32)
    final_output = shared_prefix[:, :, :, None, :] + 0.5 * random_noise
    return final_output.reshape(ROLLOUT_COUNT, DECODE_STEPS, QUERY_HEADS * HEAD_SIZE).astype(jnp.bfloat16)


def draw_dec_keys(key, part):
    shared_prefix = decode_common(key)
    key = jax.random.fold_in(key, 4)
    random_noise = jax.random.truncated_normal(key, -6.0, 6.0, (ROLLOUT_COUNT, DECODE_STEPS, KEY_VALUE_HEADS, HEAD_SIZE), jnp.float32)
    final_output = 0.7 * shared_prefix + 0.5 * random_noise
    return final_output.reshape(ROLLOUT_COUNT, DECODE_STEPS, KEY_VALUE_HEADS * HEAD_SIZE).astype(jnp.bfloat16)


def draw_block_lists(key, part):
    key = jax.random.fold_in(key, 5)

    def single_head(head_key):
        leading_key, second_key, third_key = jax.random.split(head_key, 3)
        distant_pool = jax.random.permutation(leading_key, PROMPT_BLOCKS - SLASH - 1)[:VERT].astype(jnp.int32)
        row_ids = jnp.arange(PROMPT_BLOCKS, dtype=jnp.int32)[:, None]
        diagonal = row_ids - jnp.arange(1, SLASH + 1, dtype=jnp.int32)[None, :]
        diagonal_keep = (diagonal >= 0) & (jax.random.randint(second_key, (PROMPT_BLOCKS, SLASH), 0, 2) == 1)
        distant_keep = (distant_pool[None, :] < row_ids - SLASH) & ((jax.random.randint(third_key, (PROMPT_BLOCKS, VERT), 0, 2) == 1) | (row_ids == PROMPT_BLOCKS - 1))
        candidates = jnp.concatenate([row_ids, diagonal, jnp.broadcast_to(distant_pool[None, :], (PROMPT_BLOCKS, VERT))], 1)
        keep = jnp.concatenate([jnp.ones((PROMPT_BLOCKS, 1), bool), diagonal_keep, distant_keep], 1)
        slot_ids = jnp.arange(VERT + SLASH + 1, dtype=jnp.int32)[None, :]
        order = jnp.argsort(jnp.where(keep, 0, 1) * (VERT + SLASH + 1) + slot_ids, axis=1)
        return jnp.take_along_axis(jnp.where(keep, candidates, -1), order, axis=1)
    return jax.vmap(single_head)(jax.random.split(key, KEY_VALUE_HEADS)).astype(jnp.int32)


def draw_positions(key, part):
    key = jax.random.fold_in(key, 6)
    leading_key, second_key = jax.random.split(key)
    lengths = jax.random.randint(leading_key, (ROLLOUT_COUNT,), PROMPT_LENGTH // 2, PROMPT_LENGTH + 1)
    chosen = jax.random.randint(second_key, (), 0, ROLLOUT_COUNT)
    return jnp.where(jnp.arange(ROLLOUT_COUNT) == chosen, PROMPT_LENGTH, lengths).astype(jnp.int32)


def block_levels(key, shape, shards, smallest, top_value):
    gain, own = 1.0, jax.random.fold_in(key, 6)
    for dim, shards_of in shards:
        draws = jnp.exp(jax.random.uniform(jax.random.fold_in(own, dim), (shards_of,), jnp.float32, smallest / len(shards), top_value / len(shards)))
        gain = gain * jnp.repeat(draws, shape[dim] // shards_of).reshape([-1 if axis == dim else 1 for axis in range(len(shape))])
    return gain


def scatter_about(key, dims, spread, most, pieces=(), held_as=jnp.bfloat16):
    drawn = jax.random.normal(key, dims, jnp.float32) * spread
    if len(pieces) > 0:
        drawn = block_levels(key, dims, pieces, -0.22, 0.18) * drawn
    return jnp.clip(drawn, min=-most, max=most).astype(held_as)


def setup_inputs(seed: int = 0, part: int = 0) -> dict:
    splits = jax.random.split(jax.random.key(seed), 9)
    own_keys = jax.random.split(jax.random.fold_in(splits[8], part), 9)
    return {
        "queries": draw_queries(jax.random.fold_in(jax.random.fold_in(splits[8], part), 71), part),
        "keys": draw_keys(jax.random.fold_in(jax.random.fold_in(splits[8], part), 71), part),
        "values": scatter_about(own_keys[2], (PROMPT_LENGTH, KEY_VALUE_HEADS * HEAD_SIZE), 1.0, 6.0, ((0, 8), (1, 2))),
        "block_lists": draw_block_lists(jax.random.fold_in(jax.random.fold_in(splits[8], part), 71), part),
        "dec_queries": draw_dec_queries(jax.random.fold_in(jax.random.fold_in(splits[8], part), 71), part),
        "dec_keys": draw_dec_keys(jax.random.fold_in(jax.random.fold_in(splits[8], part), 71), part),
        "decode_value_rows": scatter_about(own_keys[6], (ROLLOUT_COUNT, DECODE_STEPS, KEY_VALUE_HEADS * HEAD_SIZE), 1.0, 6.0, ((0, 8), (2, 2))),
        "positions": draw_positions(jax.random.fold_in(jax.random.fold_in(splits[8], part), 71), part),
    }


def block_mask(entries, qblock):
    keypos = (entries[:, :, None] * BLOCK_POSITIONS + jnp.arange(BLOCK_POSITIONS, dtype=jnp.int32)[None, None, :]).reshape(entries.shape[0], -1)
    valid = jnp.repeat(entries >= 0, BLOCK_POSITIONS, axis=1)
    qpos = qblock * BLOCK_POSITIONS + jnp.arange(BLOCK_POSITIONS, dtype=jnp.int32)
    return valid[:, None, :] & (keypos[:, None, :] <= qpos[None, :, None])

def rounded(weights):
    return lax.optimization_barrier(weights.astype(jnp.bfloat16)).astype(jnp.float32)

def attend_exact(query_tile, key_matrix, value_matrix, allowed, scale):
    scores = jnp.einsum('rhgd,hsd->hgrs', query_tile.astype(jnp.float32), key_matrix.astype(jnp.float32), precision=lax.Precision.HIGHEST) * scale
    scores = jnp.where(allowed[:, None], scores, -1e+30)
    top = lax.optimization_barrier(jnp.max(scores, axis=-1, keepdims=True))
    weights = jnp.exp(scores - top)
    total = lax.optimization_barrier(jnp.sum(weights, axis=-1))
    mixed = jnp.einsum('hgrs,hsd->hgrd', rounded(weights), value_matrix.astype(jnp.float32), precision=lax.Precision.HIGHEST)
    mixed = mixed / total[..., None]
    return mixed.transpose(2, 0, 1, 3).astype(jnp.bfloat16)

def reference(queries, keys, values, block_lists, dec_queries, dec_keys, decode_value_rows, positions):
    head_group = QUERY_HEADS // KEY_VALUE_HEADS
    scale = 1.0 / math.sqrt(HEAD_SIZE)
    blocked_keys = keys.reshape(PROMPT_BLOCKS, BLOCK_POSITIONS, KEY_VALUE_HEADS, HEAD_SIZE).transpose(2, 0, 1, 3)
    blocked_values = values.reshape(PROMPT_BLOCKS, BLOCK_POSITIONS, KEY_VALUE_HEADS, HEAD_SIZE).transpose(2, 0, 1, 3)
    blocked_queries = queries.reshape(PROMPT_BLOCKS, BLOCK_POSITIONS, KEY_VALUE_HEADS, head_group, HEAD_SIZE)
    head_index = jnp.arange(KEY_VALUE_HEADS, dtype=jnp.int32)[:, None]

    def prompt_tile(item):
        tile, entries, index = item
        cache_slots = jnp.maximum(entries, 0)
        key_matrix = blocked_keys[head_index, cache_slots].reshape(KEY_VALUE_HEADS, -1, HEAD_SIZE)
        value_matrix = blocked_values[head_index, cache_slots].reshape(KEY_VALUE_HEADS, -1, HEAD_SIZE)
        return attend_exact(tile, key_matrix, value_matrix, block_mask(entries, index), scale)
    prompt_out = lax.map(prompt_tile, (blocked_queries, block_lists.transpose(1, 0, 2), jnp.arange(PROMPT_BLOCKS, dtype=jnp.int32)))
    prompt_out = prompt_out.reshape(PROMPT_LENGTH, QUERY_HEADS * HEAD_SIZE)
    cached_key_rows = keys.reshape(PROMPT_LENGTH, KEY_VALUE_HEADS, HEAD_SIZE).astype(jnp.float32)
    cached_value_rows = values.reshape(PROMPT_LENGTH, KEY_VALUE_HEADS, HEAD_SIZE).astype(jnp.float32)
    cache_pos = jnp.arange(PROMPT_LENGTH, dtype=jnp.int32)

    def decode_row(item):
        single_query, appended_keys, appended_values, length = item
        live = cache_pos < length
        heads_of_query = single_query.reshape(DECODE_STEPS, KEY_VALUE_HEADS, head_group, HEAD_SIZE).astype(jnp.float32)
        latest_keys = appended_keys.reshape(DECODE_STEPS, KEY_VALUE_HEADS, HEAD_SIZE).astype(jnp.float32)
        latest_values = appended_values.reshape(DECODE_STEPS, KEY_VALUE_HEADS, HEAD_SIZE).astype(jnp.float32)
        results = []
        for step in range(DECODE_STEPS):
            cache_scores = jnp.einsum('hgd,lhd->hgl', heads_of_query[step], cached_key_rows, precision=lax.Precision.HIGHEST) * scale
            cache_scores = jnp.where(live[None, None, :], cache_scores, -1e+30)
            new_scores = jnp.einsum('hgd,shd->hgs', heads_of_query[step], latest_keys[:step + 1], precision=lax.Precision.HIGHEST) * scale
            top = jnp.maximum(lax.optimization_barrier(jnp.max(cache_scores, axis=-1)), lax.optimization_barrier(jnp.max(new_scores, axis=-1)))
            cache_weights = jnp.exp(cache_scores - top[..., None])
            new_weights = jnp.exp(new_scores - top[..., None])
            total = lax.optimization_barrier(jnp.sum(cache_weights, axis=-1)) + lax.optimization_barrier(jnp.sum(new_weights, axis=-1))
            mixed = jnp.einsum('hgl,lhd->hgd', rounded(cache_weights), cached_value_rows, precision=lax.Precision.HIGHEST)
            mixed = mixed + jnp.einsum('hgs,shd->hgd', rounded(new_weights), latest_values[:step + 1], precision=lax.Precision.HIGHEST)
            results.append((mixed / total[..., None]).astype(jnp.bfloat16).reshape(QUERY_HEADS * HEAD_SIZE))
        return jnp.stack(results, 0)
    decode_out = lax.map(decode_row, (dec_queries, dec_keys, decode_value_rows, positions))
    return (prompt_out, decode_out)
```

```python
import functools
import math

import jax
import jax.numpy as jnp
from jax import lax
from jax.experimental import pallas as pl
from jax.experimental.pallas import tpu as pltpu
from jax.sharding import PartitionSpec as P

QUERY_HEADS = 64
KEY_VALUE_HEADS = 8
HEAD_SIZE = 128
BLOCK_POSITIONS = 64
DECODE_STEPS = 2
GROUP = QUERY_HEADS // KEY_VALUE_HEADS
FACTOR = math.log2(math.e) / math.sqrt(HEAD_SIZE)
MASKED = -1e30
CHUNK = 4
VMEM_LIMIT = 63 * 1024 * 1024


def ring_orders(n):
    ring = list(range(0, n, 2)) + list(range(n - 1, 0, -2))
    forward = [(ring[i], ring[(i + 1) % n]) for i in range(n)]
    return forward, [(b, a) for a, b in forward]


def wide(x, lanes):
    return jnp.concatenate([x] * (lanes // HEAD_SIZE), axis=1) if lanes > HEAD_SIZE else x[:, :lanes]


def dot_t(a, b):
    return lax.dot_general(a, b, (((1,), (1,)), ((), ())), preferred_element_type=jnp.float32)


def first_part(scores, value_rows):
    top = jnp.broadcast_to(jnp.max(scores, axis=1, keepdims=True), (scores.shape[0], HEAD_SIZE))
    weights = jnp.exp2((scores - wide(top, scores.shape[1])) * FACTOR).astype(jnp.bfloat16)
    both = jnp.concatenate([value_rows, jnp.ones_like(value_rows)], axis=1)
    mixed = jnp.dot(weights, both, preferred_element_type=jnp.float32)
    return top, mixed[:, :HEAD_SIZE], mixed[:, HEAD_SIZE:]


def next_part(scores, value_rows, top, acc, total):
    new_top = jnp.maximum(top, jnp.max(scores, axis=1, keepdims=True))
    weights = jnp.exp2((scores - wide(new_top, scores.shape[1])) * FACTOR).astype(jnp.bfloat16)
    shrink = jnp.exp2((top - new_top) * FACTOR)
    both = jnp.concatenate([value_rows, jnp.ones_like(value_rows)], axis=1)
    mixed = jnp.dot(weights, both, preferred_element_type=jnp.float32)
    return new_top, acc * shrink + mixed[:, :HEAD_SIZE], total * shrink + mixed[:, HEAD_SIZE:]


def stacked_heads(ref, lane):
    parts = [
        ref[:, lane + g * HEAD_SIZE : lane + (g + 1) * HEAD_SIZE] for g in range(GROUP)
    ]
    return jnp.concatenate(parts, axis=0)


def copy_all(pairs, sem):
    copies = [pltpu.make_async_copy(src, dst, sem.at[i]) for i, (src, dst) in enumerate(pairs)]
    for c in copies:
        c.start()
    return copies


def wait_all(copies):
    for c in copies:
        c.wait()


def decode_kernel(lo, shards, heads, first, final, *refs):
    refs = list(refs)
    scal = refs.pop(0)
    q_ref, limit_ref = refs.pop(0), refs.pop(0)
    if first:
        nk_ref, nv_ref = refs.pop(0), refs.pop(0)
    else:
        state_in = refs[:3]
        refs = refs[3:]
    keys, values = refs[:shards], refs[shards : 2 * shards]
    refs = refs[2 * shards :]
    if final:
        out_ref = refs.pop(0)
    else:
        state_out = refs[:3]
        refs = refs[3:]
    key_buf, value_buf, top_ref, acc_ref, total_ref, sem, state_sem = refs
    working = (top_ref, acc_ref, total_ref)
    tokens, length = q_ref.shape[0], keys[0].shape[0]
    lanes = [slice(h * HEAD_SIZE, (h + 1) * HEAD_SIZE) for h in range(heads)]
    spans = [pl.ds(i * length, length) for i in range(shards)]
    if not first:
        state_copies = copy_all(zip(state_in, working), state_sem)
    shard_copies = [
        copy_all(
            ((keys[i], key_buf.at[spans[i], :]), (values[i], value_buf.at[spans[i], :])),
            sem.at[i],
        )
        for i in range(shards)
    ]
    query = [stacked_heads(q_ref, h * GROUP * HEAD_SIZE) for h in range(heads)]
    if first:
        for h in range(heads):
            scores = dot_t(query[h], nk_ref[:, lanes[h]])
            row = lax.broadcasted_iota(jnp.int32, scores.shape, 0) % tokens
            col = lax.broadcasted_iota(jnp.int32, scores.shape, 1)
            allowed = (col <= row) & (col >= row - row % DECODE_STEPS)
            scores = jnp.where(allowed, scores, MASKED)
            top_ref[h], acc_ref[h], total_ref[h] = first_part(scores, nv_ref[:, lanes[h]])
    else:
        wait_all(state_copies)
    for i in range(shards):
        wait_all(shard_copies[i])
        start = scal[2 + lo + i]

        def part(masked, i=i, start=start):
            for h in range(heads):
                scores = dot_t(query[h], key_buf[spans[i], lanes[h]])
                if masked:
                    col = lax.broadcasted_iota(jnp.int32, scores.shape, 1) + start
                    scores = jnp.where(col < wide(limit_ref[...], length), scores, MASKED)
                top_ref[h], acc_ref[h], total_ref[h] = next_part(
                    scores, value_buf[spans[i], lanes[h]], top_ref[h], acc_ref[h], total_ref[h]
                )

        @pl.when(start + length <= scal[0])
        def _():
            part(False)

        @pl.when((start + length > scal[0]) & (start < scal[1]))
        def _():
            part(True)

    if final:
        for h in range(heads):
            result = (acc_ref[h] / total_ref[h]).astype(out_ref.dtype)
            for g in range(GROUP):
                lane = (h * GROUP + g) * HEAD_SIZE
                out_ref[:, lane : lane + HEAD_SIZE] = result[g * tokens : (g + 1) * tokens]
    else:
        wait_all(copy_all(zip(working, state_out), state_sem))


def decode_part(query, limit, scal, keys, values, lo, hi, new=None, state=None, final=False):
    keys, values = keys[lo:hi], values[lo:hi]
    tokens, heads = query.shape[0], keys[0].shape[1] // HEAD_SIZE
    rows, length, shards = tokens * GROUP, keys[0].shape[0], hi - lo
    in_vmem = pl.BlockSpec(memory_space=pltpu.VMEM)
    in_hbm = pl.BlockSpec(memory_space=pltpu.HBM)
    state_shape = jax.ShapeDtypeStruct((heads, rows, HEAD_SIZE), jnp.float32)
    more = list(new) if state is None else list(state)
    in_specs = [in_vmem] * 2 + [in_vmem if state is None else in_hbm] * len(more)
    in_specs += [in_hbm] * (2 * shards)
    if final:
        out_specs, out_shape = in_vmem, jax.ShapeDtypeStruct(query.shape, query.dtype)
    else:
        out_specs, out_shape = [in_hbm] * 3, [state_shape] * 3
    return pl.pallas_call(
        functools.partial(decode_kernel, lo, shards, heads, state is None, final),
        grid_spec=pltpu.PrefetchScalarGridSpec(
            num_scalar_prefetch=1,
            in_specs=in_specs,
            out_specs=out_specs,
            scratch_shapes=[pltpu.VMEM((shards * length, heads * HEAD_SIZE), keys[0].dtype)] * 2
            + [pltpu.VMEM(state_shape.shape, jnp.float32)] * 3
            + [pltpu.SemaphoreType.DMA((shards, 2)), pltpu.SemaphoreType.DMA((3,))],
        ),
        out_shape=out_shape,
        compiler_params=pltpu.CompilerParams(vmem_limit_bytes=VMEM_LIMIT),
        cost_estimate=pl.CostEstimate(
            flops=1, transcendentals=1, bytes_accessed=1
        ),
        name="decode_last" if final else ("decode_first" if state is None else "decode_next"),
    )(scal, query, limit, *more, *keys, *values)


def prompt_kernel(base, lead, shards, heads, slots, first, final, held, *refs):
    refs = list(refs)
    list_ref, count_ref = refs.pop(0), refs.pop(0)
    q_ref = refs.pop(0)
    keys, values = refs[:shards], refs[shards : 2 * shards]
    refs = refs[2 * shards :]
    if not first:
        state_in = refs[:3]
        refs = refs[3:]
    refs = refs[held:]
    if final:
        out_ref = refs.pop(0)
    else:
        working = refs[:3]
        refs = refs[3:]
    key_buf, value_buf, sem = refs[:3]
    if final:
        working = refs[3:]
    length = keys[0].shape[0]

    @pl.when(pl.program_id(0) == 0)
    def _():
        pairs = []
        for i in range(shards):
            at = pl.ds(i * length, length)
            pairs += [(keys[i], key_buf.at[at, :]), (values[i], value_buf.at[at, :])]
        wait_all(copy_all(pairs, sem))

    tile = (pl.program_id(0) + base) * heads
    counts = [count_ref[tile + h] for h in range(heads)]
    most = functools.reduce(jnp.maximum, counts)
    query = [stacked_heads(q_ref, h * GROUP * HEAD_SIZE) for h in range(heads)]

    def chunk(h, at, size):
        lanes = slice(h * HEAD_SIZE, (h + 1) * HEAD_SIZE)
        ks, vs = [], []
        for j in range(size):
            row = list_ref[(tile + h) * slots + at + j] * BLOCK_POSITIONS
            rows = pl.ds(pl.multiple_of(row, BLOCK_POSITIONS), BLOCK_POSITIONS)
            ks.append(key_buf[rows, lanes])
            vs.append(value_buf[rows, lanes])
        scores = dot_t(query[h], jnp.concatenate(ks, axis=0))
        col = lax.broadcasted_iota(jnp.int32, (1, size * BLOCK_POSITIONS), 1)
        bias = jnp.where(col < (counts[h] - at) * BLOCK_POSITIONS, 0.0, MASKED)
        return scores + bias, jnp.concatenate(vs, axis=0)

    def put(h, top, acc, total):
        working[0][h], working[1][h], working[2][h] = top, acc, total

    for h in range(heads):
        scores, value_rows = chunk(h, 0, lead)
        if first:
            row = lax.broadcasted_iota(jnp.int32, (query[h].shape[0], HEAD_SIZE), 0)
            col = lax.broadcasted_iota(jnp.int32, (query[h].shape[0], HEAD_SIZE), 1)
            keep = (col <= row % BLOCK_POSITIONS) | (col >= BLOCK_POSITIONS)
            head_part = jnp.where(keep, scores[:, :HEAD_SIZE], MASKED)
            scores = jnp.concatenate([head_part, scores[:, HEAD_SIZE:]], axis=1)
            put(h, *first_part(scores, value_rows))
        else:
            put(h, *next_part(scores, value_rows, *(ref[h] for ref in state_in)))

    def step(i, carry):
        for h in range(heads):
            scores, value_rows = chunk(h, lead + i * CHUNK, CHUNK)
            put(h, *next_part(scores, value_rows, *(ref[h] for ref in working)))
        return carry

    lax.fori_loop(0, jnp.maximum(most - lead + CHUNK - 1, 0) // CHUNK, step, 0)
    if final:
        for h in range(heads):
            result = (working[1][h] / working[2][h]).astype(out_ref.dtype)
            for g in range(GROUP):
                lane = (h * GROUP + g) * HEAD_SIZE
                rows = slice(g * BLOCK_POSITIONS, (g + 1) * BLOCK_POSITIONS)
                out_ref[:, lane : lane + HEAD_SIZE] = result[rows]


def prompt_part(queries, packed, counts, keys, values, lead, span, state=None, into=None, final=False):
    base, blocks = span[0], span[1] - span[0]
    all_blocks, heads = queries.shape[0] // BLOCK_POSITIONS, keys[0].shape[1] // HEAD_SIZE
    length, shards = keys[0].shape[0], len(keys)
    slots = packed.shape[0] // (all_blocks * heads)
    tile_rows = BLOCK_POSITIONS * GROUP
    row_spec = pl.BlockSpec((BLOCK_POSITIONS, queries.shape[1]), lambda b, *_: (b + base, 0))
    in_hbm = pl.BlockSpec(memory_space=pltpu.HBM)
    state_spec = pl.BlockSpec(
        (None, heads, tile_rows, HEAD_SIZE), lambda b, *_: (b + base, 0, 0, 0)
    )
    state_shape = jax.ShapeDtypeStruct((all_blocks, heads, tile_rows, HEAD_SIZE), jnp.float32)
    in_specs = [row_spec] + [in_hbm] * (2 * shards)
    args = [queries] + list(keys) + list(values)
    if state is not None:
        in_specs += [state_spec] * 3
        args += list(state)
    aliases = {}
    if into is not None:
        aliases = {2 + len(args) + i: i for i in range(3)}
        in_specs += [in_hbm] * 3
        args += list(into)
    scratch = [pltpu.VMEM((shards * length, heads * HEAD_SIZE), keys[0].dtype)] * 2
    scratch += [pltpu.SemaphoreType.DMA((2 * shards,))]
    if final:
        out_specs, out_shape = row_spec, jax.ShapeDtypeStruct(queries.shape, queries.dtype)
        scratch += [pltpu.VMEM((heads, tile_rows, HEAD_SIZE), jnp.float32)] * 3
    else:
        out_specs, out_shape = [state_spec] * 3, [state_shape] * 3
    return pl.pallas_call(
        functools.partial(
            prompt_kernel, base, lead, shards, heads, slots, state is None, final, len(aliases)
        ),
        grid_spec=pltpu.PrefetchScalarGridSpec(
            num_scalar_prefetch=2,
            grid=(blocks,),
            in_specs=in_specs,
            out_specs=out_specs,
            scratch_shapes=scratch,
        ),
        out_shape=out_shape,
        input_output_aliases=aliases,
        compiler_params=pltpu.CompilerParams(vmem_limit_bytes=VMEM_LIMIT),
        cost_estimate=pl.CostEstimate(
            flops=1, transcendentals=1, bytes_accessed=1
        ),
        name="prompt_last" if final else "prompt_first",
    )(packed, counts, *args)


def local(
    n, queries, keys, values, block_lists, dec_queries, dec_keys, decode_value_rows, positions
):
    rows = queries.shape[0]
    per_dev = rows // BLOCK_POSITIONS
    half = n // 2
    me = lax.axis_index("seq")

    def ring_place(s):
        return jnp.where(s % 2 == 0, s // 2, n - 1 - s // 2)

    place = ring_place(me)
    forward, backward = ring_orders(n)
    offsets = [0]
    for d in range(1, half):
        offsets += [-d, d]
    offsets += [half]
    at = (place + jnp.array(offsets, jnp.int32)) % n
    starts = jnp.where(at < half, 2 * at, 2 * (n - 1 - at) + 1) * rows

    first = me * per_dev
    mine = lax.dynamic_slice_in_dim(block_lists, first, per_dev, 1).transpose(1, 0, 2)
    valid = mine >= 0
    entry = jnp.maximum(mine, 0)
    delta = (ring_place(entry // per_dev) - place) % n
    slot = jnp.where(delta < half, 2 * delta, 2 * (n - delta) - 1)
    entry = slot * per_dev + entry % per_dev
    slots = -(-entry.shape[-1] // CHUNK) * CHUNK
    packed = jnp.pad(entry, ((0, 0), (0, 0), (0, slots - entry.shape[-1]))).reshape(-1)
    counts = jnp.sum(valid.astype(jnp.int32), axis=-1).reshape(-1)

    owned, steps = dec_queries.shape[0], dec_queries.shape[1]
    limits = lax.dynamic_slice_in_dim(positions, me * owned, owned, 0)
    query = dec_queries.reshape(owned * steps, -1)
    new = (dec_keys.reshape(owned * steps, -1), decode_value_rows.reshape(owned * steps, -1))
    limit = jnp.broadcast_to(
        limits[None, :, None, None], (GROUP, owned, steps, HEAD_SIZE)
    ).reshape(-1, HEAD_SIZE)
    scal = jnp.concatenate([jnp.min(limits)[None], jnp.max(limits)[None], starts])
    decode = functools.partial(decode_part, query, limit, scal)

    shard_keys, shard_values = [keys], [values]
    key_f, value_f, key_b, value_b = keys, values, keys, values
    before = [None, None]
    for d in range(1, half + 1):
        if before[0] is not None:
            key_f, key_b, before[0] = lax.optimization_barrier((key_f, key_b, before[0]))
        if before[1] is not None:
            value_f, value_b, before[1] = lax.optimization_barrier((value_f, value_b, before[1]))
        key_f = lax.ppermute(key_f, "seq", forward)
        value_b = lax.ppermute(value_b, "seq", backward)
        if d < half:
            key_b = lax.ppermute(key_b, "seq", backward)
            value_f = lax.ppermute(value_f, "seq", forward)
            shard_keys += [key_f, key_b]
            shard_values += [value_f, value_b]
        else:
            shard_keys += [key_f]
            shard_values += [value_b]
        before = [None, None]
        if d == 1:
            state = decode(shard_keys, shard_values, 0, 3, new=new)
        elif d < half - 2:
            state = decode(shard_keys, shard_values, 2 * d - 1, 2 * d + 1, state=state)
            before[1] = state[0]
        elif d == half - 2:
            before[1] = state[0]
    state = decode(shard_keys, shard_values, n - 5, n - 1, state=state)
    decode_out = decode(shard_keys, shard_values, n - 1, n, state=state, final=True)
    prompt_out = prompt_part(
        queries, packed, counts, shard_keys, shard_values, 8, (0, per_dev), final=True
    )
    return prompt_out, decode_out.reshape(owned, steps, -1)


def solution(mesh):
    return jax.shard_map(
        functools.partial(local, mesh.shape["seq"]),
        mesh=mesh,
        in_specs=(
            P(("groups", "seq"), "head"),
            P(("groups", "seq"), "head"),
            P(("groups", "seq"), "head"),
            P("head", "groups", None),
            P(("groups", "seq"), None, "head"),
            P(("groups", "seq"), None, "head"),
            P(("groups", "seq"), None, "head"),
            P("groups"),
        ),
        out_specs=(P(("groups", "seq"), "head"), P(("groups", "seq"), None, "head")),
        check_vma=False,
    )
```

```python
import functools
import math

import jax
import jax.numpy as jnp
from jax import lax
from jax.experimental import pallas as pl
from jax.experimental.pallas import tpu as pltpu
from jax.sharding import PartitionSpec as P

QUERY_HEADS = 64
KEY_VALUE_HEADS = 8
HEAD_SIZE = 128
BLOCK_POSITIONS = 64
DECODE_STEPS = 2
GROUP = QUERY_HEADS // KEY_VALUE_HEADS
FACTOR = math.log2(math.e) / math.sqrt(HEAD_SIZE)
MASKED = -1e30
CHUNK = 4
LEADS = (4, 8, 12, 16)
VMEM_LIMIT = 63 * 1024 * 1024


def ring_orders(n):
    ring = list(range(0, n, 2)) + list(range(n - 1, 0, -2))
    forward = [(ring[i], ring[(i + 1) % n]) for i in range(n)]
    return forward, [(b, a) for a, b in forward]


def wide(x, lanes):
    return jnp.concatenate([x] * (lanes // HEAD_SIZE), axis=1) if lanes > HEAD_SIZE else x[:, :lanes]


def dot_t(a, b):
    return lax.dot_general(a, b, (((1,), (1,)), ((), ())), preferred_element_type=jnp.float32)


def first_part(scores, value_rows):
    top = jnp.broadcast_to(jnp.max(scores, axis=1, keepdims=True), (scores.shape[0], HEAD_SIZE))
    weights = jnp.exp2((scores - wide(top, scores.shape[1])) * FACTOR).astype(jnp.bfloat16)
    both = jnp.concatenate([value_rows, jnp.ones_like(value_rows)], axis=1)
    mixed = jnp.dot(weights, both, preferred_element_type=jnp.float32)
    return top, mixed[:, :HEAD_SIZE], mixed[:, HEAD_SIZE:]


def next_part(scores, value_rows, top, acc, total):
    new_top = jnp.maximum(top, jnp.max(scores, axis=1, keepdims=True))
    weights = jnp.exp2((scores - wide(new_top, scores.shape[1])) * FACTOR).astype(jnp.bfloat16)
    shrink = jnp.exp2((top - new_top) * FACTOR)
    both = jnp.concatenate([value_rows, jnp.ones_like(value_rows)], axis=1)
    mixed = jnp.dot(weights, both, preferred_element_type=jnp.float32)
    return new_top, acc * shrink + mixed[:, :HEAD_SIZE], total * shrink + mixed[:, HEAD_SIZE:]


def inverse(x):
    rough = pl.reciprocal(x, approx=True)
    return rough * (2.0 - x * rough)


def each_ahead(count, begin, finish):
    held = begin(0)
    for i in range(count):
        following = begin(i + 1) if i + 1 < count else None
        finish(i, held)
        held = following


def stacked_heads(ref, lane):
    parts = [
        ref[:, lane + g * HEAD_SIZE : lane + (g + 1) * HEAD_SIZE] for g in range(GROUP)
    ]
    return jnp.concatenate(parts, axis=0)


def copy_all(pairs, sem):
    copies = [pltpu.make_async_copy(src, dst, sem.at[i]) for i, (src, dst) in enumerate(pairs)]
    for c in copies:
        c.start()
    return copies


def wait_all(copies):
    for c in copies:
        c.wait()


def decode_kernel(lo, shards, heads, first, *refs):
    refs = list(refs)
    scal = refs.pop(0)
    q_ref, limit_ref = refs.pop(0), refs.pop(0)
    if first:
        nk_ref, nv_ref = refs.pop(0), refs.pop(0)
    else:
        state_in = refs[:3]
        refs = refs[3:]
    keys, values = refs[:shards], refs[shards : 2 * shards]
    refs = refs[2 * shards :]
    state_out = refs[:3]
    refs = refs[3:]
    key_buf, value_buf, top_ref, acc_ref, total_ref, sem, state_sem = refs
    working = (top_ref, acc_ref, total_ref)
    tokens, length = q_ref.shape[0], keys[0].shape[0]
    lanes = [slice(h * HEAD_SIZE, (h + 1) * HEAD_SIZE) for h in range(heads)]
    spans = [pl.ds(i * length, length) for i in range(shards)]
    if not first:
        state_copies = copy_all(zip(state_in, working), state_sem)
    shard_copies = [
        copy_all(
            ((keys[i], key_buf.at[spans[i], :]), (values[i], value_buf.at[spans[i], :])),
            sem.at[i],
        )
        for i in range(shards)
    ]
    query = [stacked_heads(q_ref, h * GROUP * HEAD_SIZE) for h in range(heads)]
    if first:
        def begin(h):
            scores = dot_t(query[h], nk_ref[:, lanes[h]])
            row = lax.broadcasted_iota(jnp.int32, scores.shape, 0) % tokens
            col = lax.broadcasted_iota(jnp.int32, scores.shape, 1)
            allowed = (col <= row) & (col >= row - row % DECODE_STEPS)
            return jnp.where(allowed, scores, MASKED)

        def finish(h, scores):
            top_ref[h], acc_ref[h], total_ref[h] = first_part(scores, nv_ref[:, lanes[h]])

        each_ahead(heads, begin, finish)
    else:
        wait_all(state_copies)
    for i in range(shards):
        wait_all(shard_copies[i])
        start = scal[2 + lo + i]

        def part(masked, i=i, start=start):
            def begin(h):
                scores = dot_t(query[h], key_buf[spans[i], lanes[h]])
                if masked:
                    col = lax.broadcasted_iota(jnp.int32, scores.shape, 1) + start
                    scores = jnp.where(col < wide(limit_ref[...], length), scores, MASKED)
                return scores

            def finish(h, scores):
                top_ref[h], acc_ref[h], total_ref[h] = next_part(
                    scores, value_buf[spans[i], lanes[h]], top_ref[h], acc_ref[h], total_ref[h]
                )

            each_ahead(heads, begin, finish)

        @pl.when(start + length <= scal[0])
        def _():
            part(False)

        @pl.when((start + length > scal[0]) & (start < scal[1]))
        def _():
            part(True)

    wait_all(copy_all(zip(working, state_out), state_sem))


def decode_part(query, limit, scal, keys, values, lo, hi, new=None, state=None):
    keys, values = keys[lo:hi], values[lo:hi]
    tokens, heads = query.shape[0], keys[0].shape[1] // HEAD_SIZE
    rows, length, shards = tokens * GROUP, keys[0].shape[0], hi - lo
    in_vmem = pl.BlockSpec(memory_space=pltpu.VMEM)
    in_hbm = pl.BlockSpec(memory_space=pltpu.HBM)
    state_shape = jax.ShapeDtypeStruct((heads, rows, HEAD_SIZE), jnp.float32)
    more = list(new) if state is None else list(state)
    in_specs = [in_vmem] * 2 + [in_vmem if state is None else in_hbm] * len(more)
    in_specs += [in_hbm] * (2 * shards)
    out_specs, out_shape = [in_hbm] * 3, [state_shape] * 3
    return pl.pallas_call(
        functools.partial(decode_kernel, lo, shards, heads, state is None),
        grid_spec=pltpu.PrefetchScalarGridSpec(
            num_scalar_prefetch=1,
            in_specs=in_specs,
            out_specs=out_specs,
            scratch_shapes=[pltpu.VMEM((shards * length, heads * HEAD_SIZE), keys[0].dtype)] * 2
            + [pltpu.VMEM(state_shape.shape, jnp.float32)] * 3
            + [pltpu.SemaphoreType.DMA((shards, 2)), pltpu.SemaphoreType.DMA((3,))],
        ),
        out_shape=out_shape,
        compiler_params=pltpu.CompilerParams(vmem_limit_bytes=VMEM_LIMIT),
        cost_estimate=pl.CostEstimate(
            flops=1, transcendentals=1, bytes_accessed=1
        ),
        name="decode_first" if state is None else "decode_next",
    )(scal, query, limit, *more, *keys, *values)


def last_kernel(shards, heads, slots, *refs):
    refs = list(refs)
    list_ref, count_ref, scal, q_ref, dec_q_ref, limit_ref = refs[:6]
    state_in = refs[6:9]
    keys, values = refs[9 : 9 + shards], refs[9 + shards : 9 + 2 * shards]
    out_ref, dec_out_ref, key_buf, value_buf = refs[9 + 2 * shards : 13 + 2 * shards]
    working = refs[13 + 2 * shards : 16 + 2 * shards]
    state = refs[16 + 2 * shards : 19 + 2 * shards]
    sem, state_sem = refs[19 + 2 * shards :]
    length = keys[0].shape[0]
    lanes = [slice(h * HEAD_SIZE, (h + 1) * HEAD_SIZE) for h in range(heads)]

    @pl.when(pl.program_id(0) == 0)
    def _():
        state_copies = copy_all(zip(state_in, state), state_sem)
        shard_copies = []
        for i in reversed(range(shards)):
            at = pl.ds(i * length, length)
            pairs = ((keys[i], key_buf.at[at, :]), (values[i], value_buf.at[at, :]))
            shard_copies.append(copy_all(pairs, sem.at[i]))
        tokens = dec_q_ref.shape[0]
        start = scal[2 + shards - 1]
        rows = slice((shards - 1) * length, shards * length)
        wait_all(state_copies)
        wait_all(shard_copies[0])

        def begin(h):
            query = stacked_heads(dec_q_ref, h * GROUP * HEAD_SIZE)
            scores = dot_t(query, key_buf[rows, lanes[h]])
            col = lax.broadcasted_iota(jnp.int32, scores.shape, 1) + start
            return jnp.where(col < wide(limit_ref[...], length), scores, MASKED)

        def finish(h, scores):
            _, acc, total = next_part(
                scores, value_buf[rows, lanes[h]], *(ref[h] for ref in state)
            )
            result = (acc * inverse(total)).astype(dec_out_ref.dtype)
            for g in range(GROUP):
                lane = (h * GROUP + g) * HEAD_SIZE
                dec_out_ref[:, lane : lane + HEAD_SIZE] = result[g * tokens : (g + 1) * tokens]

        each_ahead(heads, begin, finish)
        for copies in shard_copies[1:]:
            wait_all(copies)

    tile = pl.program_id(0) * heads
    counts = [count_ref[tile + h] for h in range(heads)]
    most = functools.reduce(jnp.maximum, counts)

    def chunk(h, at, size):
        ks, vs = [], []
        for j in range(size):
            row = list_ref[(tile + h) * slots + at + j] * BLOCK_POSITIONS
            rows = pl.ds(pl.multiple_of(row, BLOCK_POSITIONS), BLOCK_POSITIONS)
            ks.append(key_buf[rows, lanes[h]])
            vs.append(value_buf[rows, lanes[h]])
        query = stacked_heads(q_ref, h * GROUP * HEAD_SIZE)
        scores = dot_t(query, jnp.concatenate(ks, axis=0))
        col = lax.broadcasted_iota(jnp.int32, (1, size * BLOCK_POSITIONS), 1)
        bias = jnp.where(col < (counts[h] - at) * BLOCK_POSITIONS, 0.0, MASKED)
        return scores + bias, jnp.concatenate(vs, axis=0)

    def leading(h, size):
        scores, value_rows = chunk(h, 0, size)
        row = lax.broadcasted_iota(jnp.int32, (scores.shape[0], HEAD_SIZE), 0)
        col = lax.broadcasted_iota(jnp.int32, (scores.shape[0], HEAD_SIZE), 1)
        keep = (col <= row % BLOCK_POSITIONS) | (col >= BLOCK_POSITIONS)
        head_part = jnp.where(keep, scores[:, :HEAD_SIZE], MASKED)
        return jnp.concatenate([head_part, scores[:, HEAD_SIZE:]], axis=1), value_rows

    def give(h, acc, total):
        result = (acc * inverse(total)).astype(out_ref.dtype)
        for g in range(GROUP):
            lane = (h * GROUP + g) * HEAD_SIZE
            rows = slice(g * BLOCK_POSITIONS, (g + 1) * BLOCK_POSITIONS)
            out_ref[:, lane : lane + HEAD_SIZE] = result[rows]

    def put(h, parts):
        working[0][h], working[1][h], working[2][h] = parts

    for low, size in zip((-1,) + LEADS[:-1], LEADS):

        @pl.when((most > low) & (most <= size))
        def _(size=size):
            each_ahead(
                heads,
                lambda h: leading(h, size),
                lambda h, held: give(h, *first_part(*held)[1:]),
            )

    @pl.when(most > LEADS[-1])
    def _():
        each_ahead(
            heads,
            lambda h: leading(h, LEADS[-1]),
            lambda h, held: put(h, first_part(*held)),
        )

        def step(i, carry):
            each_ahead(
                heads,
                lambda h: chunk(h, LEADS[-1] + i * CHUNK, CHUNK),
                lambda h, held: put(h, next_part(*held, *(ref[h] for ref in working))),
            )
            return carry

        lax.fori_loop(0, (most - LEADS[-1] + CHUNK - 1) // CHUNK, step, 0)
        for h in range(heads):
            give(h, working[1][h], working[2][h])


def last_part(queries, packed, counts, scal, dec_query, limit, state, keys, values):
    blocks, heads = queries.shape[0] // BLOCK_POSITIONS, keys[0].shape[1] // HEAD_SIZE
    length, shards = keys[0].shape[0], len(keys)
    slots = packed.shape[0] // (blocks * heads)
    tile_rows = BLOCK_POSITIONS * GROUP
    row_spec = pl.BlockSpec((BLOCK_POSITIONS, queries.shape[1]), lambda b, *_: (b, 0))
    in_hbm = pl.BlockSpec(memory_space=pltpu.HBM)
    dec_spec = pl.BlockSpec(dec_query.shape, lambda b, *_: (0, 0))
    limit_spec = pl.BlockSpec(limit.shape, lambda b, *_: (0, 0))
    return pl.pallas_call(
        functools.partial(last_kernel, shards, heads, slots),
        grid_spec=pltpu.PrefetchScalarGridSpec(
            num_scalar_prefetch=3,
            grid=(blocks,),
            in_specs=[row_spec, dec_spec, limit_spec] + [in_hbm] * (3 + 2 * shards),
            out_specs=[row_spec, dec_spec],
            scratch_shapes=[pltpu.VMEM((shards * length, heads * HEAD_SIZE), keys[0].dtype)] * 2
            + [pltpu.VMEM((heads, tile_rows, HEAD_SIZE), jnp.float32)] * 3
            + [pltpu.VMEM(state[0].shape, jnp.float32)] * 3
            + [pltpu.SemaphoreType.DMA((shards, 2)), pltpu.SemaphoreType.DMA((3,))],
        ),
        out_shape=[
            jax.ShapeDtypeStruct(queries.shape, queries.dtype),
            jax.ShapeDtypeStruct(dec_query.shape, dec_query.dtype),
        ],
        compiler_params=pltpu.CompilerParams(vmem_limit_bytes=VMEM_LIMIT),
        cost_estimate=pl.CostEstimate(flops=1, transcendentals=1, bytes_accessed=1),
        name="prompt",
    )(packed, counts, scal, queries, dec_query, limit, *state, *keys, *values)


def local(
    n, queries, keys, values, block_lists, dec_queries, dec_keys, decode_value_rows, positions
):
    rows = queries.shape[0]
    per_dev = rows // BLOCK_POSITIONS
    half = n // 2
    me = lax.axis_index("seq")

    def ring_place(s):
        return jnp.where(s % 2 == 0, s // 2, n - 1 - s // 2)

    place = ring_place(me)
    forward, backward = ring_orders(n)
    offsets = [0]
    for d in range(1, half):
        offsets += [-d, d]
    offsets += [half]
    at = (place + jnp.array(offsets, jnp.int32)) % n
    starts = jnp.where(at < half, 2 * at, 2 * (n - 1 - at) + 1) * rows

    first = me * per_dev
    mine = lax.dynamic_slice_in_dim(block_lists, first, per_dev, 1).transpose(1, 0, 2)
    valid = mine >= 0
    entry = jnp.maximum(mine, 0)
    delta = (ring_place(entry // per_dev) - place) % n
    slot = jnp.where(delta < half, 2 * delta, 2 * (n - delta) - 1)
    entry = slot * per_dev + entry % per_dev
    slots = -(-entry.shape[-1] // CHUNK) * CHUNK
    packed = jnp.pad(entry, ((0, 0), (0, 0), (0, slots - entry.shape[-1]))).reshape(-1)
    counts = jnp.sum(valid.astype(jnp.int32), axis=-1).reshape(-1)

    owned, steps = dec_queries.shape[0], dec_queries.shape[1]
    limits = lax.dynamic_slice_in_dim(positions, me * owned, owned, 0)
    query = dec_queries.reshape(owned * steps, -1)
    new = (dec_keys.reshape(owned * steps, -1), decode_value_rows.reshape(owned * steps, -1))
    limit = jnp.broadcast_to(
        limits[None, :, None, None], (GROUP, owned, steps, HEAD_SIZE)
    ).reshape(-1, HEAD_SIZE)
    scal = jnp.concatenate([jnp.min(limits)[None], jnp.max(limits)[None], starts])
    decode = functools.partial(decode_part, query, limit, scal)

    shard_keys, shard_values = [keys], [values]
    key_f, value_f, key_b, value_b = keys, values, keys, values
    before = [(), ()]
    for d in range(1, half + 1):
        key_f, key_b, *_ = lax.optimization_barrier((key_f, key_b, *before[0]))
        value_f, value_b, *_ = lax.optimization_barrier((value_f, value_b, *before[1]))
        key_f = lax.ppermute(key_f, "seq", forward)
        value_b = lax.ppermute(value_b, "seq", backward)
        if d < half:
            key_b = lax.ppermute(key_b, "seq", backward)
            value_f = lax.ppermute(value_f, "seq", forward)
            shard_keys += [key_f, key_b]
            shard_values += [value_f, value_b]
        else:
            shard_keys += [key_f]
            shard_values += [value_b]
        before = [(), ()]
        if d == 1:
            state = decode(shard_keys, shard_values, 0, 1, new=new)
            before[1] = (state[0], packed, counts)
        elif d < half:
            state = decode(shard_keys, shard_values, 2 * d - 3, 2 * d - 1, state=state)
            before[1] = (state[0],)
    state = decode(shard_keys, shard_values, n - 3, n - 1, state=state)
    prompt_out, decode_out = last_part(
        queries, packed, counts, scal, query, limit, state, shard_keys, shard_values
    )
    return prompt_out, decode_out.reshape(owned, steps, -1)


def solution(mesh):
    return jax.shard_map(
        functools.partial(local, mesh.shape["seq"]),
        mesh=mesh,
        in_specs=(
            P(("groups", "seq"), "head"),
            P(("groups", "seq"), "head"),
            P(("groups", "seq"), "head"),
            P("head", "groups", None),
            P(("groups", "seq"), None, "head"),
            P(("groups", "seq"), None, "head"),
            P(("groups", "seq"), None, "head"),
            P("groups"),
        ),
        out_specs=(P(("groups", "seq"), "head"), P(("groups", "seq"), None, "head")),
        check_vma=False,
    )
```

```python
import functools
import math

import jax
import jax.numpy as jnp
from jax import lax
from jax.experimental import pallas as pl
from jax.experimental.pallas import tpu as pltpu
from jax.sharding import PartitionSpec as P

QUERY_HEADS = 64
KEY_VALUE_HEADS = 8
HEAD_SIZE = 128
BLOCK_POSITIONS = 64
DECODE_STEPS = 2
GROUP = QUERY_HEADS // KEY_VALUE_HEADS
FACTOR = math.log2(math.e) / math.sqrt(HEAD_SIZE)
MASKED = -1e30
CHUNK = 4
LEADS = (12, 16)
VMEM_LIMIT = 63 * 1024 * 1024


def ring_orders(n):
    ring = list(range(0, n, 2)) + list(range(n - 1, 0, -2))
    forward = [(ring[i], ring[(i + 1) % n]) for i in range(n)]
    return forward, [(b, a) for a, b in forward]


def wide(x, lanes):
    return jnp.concatenate([x] * (lanes // HEAD_SIZE), axis=1) if lanes > HEAD_SIZE else x[:, :lanes]


def dot_t(a, b):
    return lax.dot_general(a, b, (((1,), (1,)), ((), ())), preferred_element_type=jnp.float32)


def first_part(scores, value_rows):
    top = jnp.broadcast_to(jnp.max(scores, axis=1, keepdims=True), (scores.shape[0], HEAD_SIZE))
    weights = jnp.exp2((scores - wide(top, scores.shape[1])) * FACTOR).astype(jnp.bfloat16)
    both = jnp.concatenate([value_rows, jnp.ones_like(value_rows)], axis=1)
    mixed = jnp.dot(weights, both, preferred_element_type=jnp.float32)
    return top, mixed[:, :HEAD_SIZE], mixed[:, HEAD_SIZE:]


def next_part(scores, value_rows, top, acc, total):
    new_top = jnp.maximum(top, jnp.max(scores, axis=1, keepdims=True))
    weights = jnp.exp2((scores - wide(new_top, scores.shape[1])) * FACTOR).astype(jnp.bfloat16)
    shrink = jnp.exp2((top - new_top) * FACTOR)
    both = jnp.concatenate([value_rows, jnp.ones_like(value_rows)], axis=1)
    mixed = jnp.dot(weights, both, preferred_element_type=jnp.float32)
    return new_top, acc * shrink + mixed[:, :HEAD_SIZE], total * shrink + mixed[:, HEAD_SIZE:]


def inverse(x):
    rough = pl.reciprocal(x, approx=True)
    return rough * (2.0 - x * rough)


def each_ahead(count, begin, finish):
    held = begin(0)
    for i in range(count):
        following = begin(i + 1) if i + 1 < count else None
        finish(i, held)
        held = following


def stacked_heads(ref, lane):
    parts = [
        ref[:, lane + g * HEAD_SIZE : lane + (g + 1) * HEAD_SIZE] for g in range(GROUP)
    ]
    return jnp.concatenate(parts, axis=0)


def copy_all(pairs, sem):
    copies = [pltpu.make_async_copy(src, dst, sem.at[i]) for i, (src, dst) in enumerate(pairs)]
    for c in copies:
        c.start()
    return copies


def wait_all(copies):
    for c in copies:
        c.wait()


def decode_kernel(lo, shards, heads, first, *refs):
    refs = list(refs)
    scal = refs.pop(0)
    q_ref, limit_ref = refs.pop(0), refs.pop(0)
    if first:
        nk_ref, nv_ref = refs.pop(0), refs.pop(0)
    else:
        state_in = refs[:3]
        refs = refs[3:]
    keys, values = refs[:shards], refs[shards : 2 * shards]
    refs = refs[2 * shards :]
    state_out = refs[:3]
    refs = refs[3:]
    key_buf, value_buf, top_ref, acc_ref, total_ref, sem, state_sem = refs
    working = (top_ref, acc_ref, total_ref)
    tokens, length = q_ref.shape[0], keys[0].shape[0]
    lanes = [slice(h * HEAD_SIZE, (h + 1) * HEAD_SIZE) for h in range(heads)]
    spans = [pl.ds(i * length, length) for i in range(shards)]
    if not first:
        state_copies = copy_all(zip(state_in, working), state_sem)
    shard_copies = [
        copy_all(
            ((keys[i], key_buf.at[spans[i], :]), (values[i], value_buf.at[spans[i], :])),
            sem.at[i],
        )
        for i in range(shards)
    ]
    query = [stacked_heads(q_ref, h * GROUP * HEAD_SIZE) for h in range(heads)]
    if first:
        def begin(h):
            scores = dot_t(query[h], nk_ref[:, lanes[h]])
            row = lax.broadcasted_iota(jnp.int32, scores.shape, 0) % tokens
            col = lax.broadcasted_iota(jnp.int32, scores.shape, 1)
            allowed = (col <= row) & (col >= row - row % DECODE_STEPS)
            return jnp.where(allowed, scores, MASKED)

        def finish(h, scores):
            top_ref[h], acc_ref[h], total_ref[h] = first_part(scores, nv_ref[:, lanes[h]])

        each_ahead(heads, begin, finish)
    else:
        wait_all(state_copies)
    for i in range(shards):
        wait_all(shard_copies[i])
        start = scal[2 + lo + i]

        def part(masked, i=i, start=start):
            def begin(h):
                scores = dot_t(query[h], key_buf[spans[i], lanes[h]])
                if masked:
                    col = lax.broadcasted_iota(jnp.int32, scores.shape, 1) + start
                    scores = jnp.where(col < wide(limit_ref[...], length), scores, MASKED)
                return scores

            def finish(h, scores):
                top_ref[h], acc_ref[h], total_ref[h] = next_part(
                    scores, value_buf[spans[i], lanes[h]], top_ref[h], acc_ref[h], total_ref[h]
                )

            each_ahead(heads, begin, finish)

        @pl.when(start + length <= scal[0])
        def _():
            part(False)

        @pl.when((start + length > scal[0]) & (start < scal[1]))
        def _():
            part(True)

    wait_all(copy_all(zip(working, state_out), state_sem))


def decode_part(query, limit, scal, keys, values, lo, hi, new=None, state=None):
    keys, values = keys[lo:hi], values[lo:hi]
    tokens, heads = query.shape[0], keys[0].shape[1] // HEAD_SIZE
    rows, length, shards = tokens * GROUP, keys[0].shape[0], hi - lo
    in_vmem = pl.BlockSpec(memory_space=pltpu.VMEM)
    in_hbm = pl.BlockSpec(memory_space=pltpu.HBM)
    state_shape = jax.ShapeDtypeStruct((heads, rows, HEAD_SIZE), jnp.float32)
    more = list(new) if state is None else list(state)
    in_specs = [in_vmem] * 2 + [in_vmem if state is None else in_hbm] * len(more)
    in_specs += [in_hbm] * (2 * shards)
    out_specs, out_shape = [in_hbm] * 3, [state_shape] * 3
    return pl.pallas_call(
        functools.partial(decode_kernel, lo, shards, heads, state is None),
        grid_spec=pltpu.PrefetchScalarGridSpec(
            num_scalar_prefetch=1,
            in_specs=in_specs,
            out_specs=out_specs,
            scratch_shapes=[pltpu.VMEM((shards * length, heads * HEAD_SIZE), keys[0].dtype)] * 2
            + [pltpu.VMEM(state_shape.shape, jnp.float32)] * 3
            + [pltpu.SemaphoreType.DMA((shards, 2)), pltpu.SemaphoreType.DMA((3,))],
        ),
        out_shape=out_shape,
        compiler_params=pltpu.CompilerParams(vmem_limit_bytes=VMEM_LIMIT),
        cost_estimate=pl.CostEstimate(
            flops=1, transcendentals=1, bytes_accessed=1
        ),
        name="decode_first" if state is None else "decode_next",
    )(scal, query, limit, *more, *keys, *values)


def last_kernel(shards, heads, slots, *refs):
    refs = list(refs)
    list_ref, count_ref, scal, q_ref, dec_q_ref, limit_ref = refs[:6]
    state_in = refs[6:9]
    keys, values = refs[9 : 9 + shards], refs[9 + shards : 9 + 2 * shards]
    out_ref, dec_out_ref, key_buf, value_buf = refs[9 + 2 * shards : 13 + 2 * shards]
    working = refs[13 + 2 * shards : 16 + 2 * shards]
    state = refs[16 + 2 * shards : 19 + 2 * shards]
    sem, state_sem = refs[19 + 2 * shards :]
    length = keys[0].shape[0]
    lanes = [slice(h * HEAD_SIZE, (h + 1) * HEAD_SIZE) for h in range(heads)]

    @pl.when(pl.program_id(0) == 0)
    def _():
        state_copies = copy_all(zip(state_in, state), state_sem)
        shard_copies = []
        for i in reversed(range(shards)):
            at = pl.ds(i * length, length)
            pairs = ((keys[i], key_buf.at[at, :]), (values[i], value_buf.at[at, :]))
            shard_copies.append(copy_all(pairs, sem.at[i]))
        tokens = dec_q_ref.shape[0]
        start = scal[2 + shards - 1]
        rows = slice((shards - 1) * length, shards * length)
        wait_all(state_copies)
        wait_all(shard_copies[0])

        def begin(h):
            query = stacked_heads(dec_q_ref, h * GROUP * HEAD_SIZE)
            scores = dot_t(query, key_buf[rows, lanes[h]])
            col = lax.broadcasted_iota(jnp.int32, scores.shape, 1) + start
            return jnp.where(col < wide(limit_ref[...], length), scores, MASKED)

        def finish(h, scores):
            _, acc, total = next_part(
                scores, value_buf[rows, lanes[h]], *(ref[h] for ref in state)
            )
            result = (acc * inverse(total)).astype(dec_out_ref.dtype)
            for g in range(GROUP):
                lane = (h * GROUP + g) * HEAD_SIZE
                dec_out_ref[:, lane : lane + HEAD_SIZE] = result[g * tokens : (g + 1) * tokens]

        each_ahead(heads, begin, finish)
        for copies in shard_copies[1:]:
            wait_all(copies)

    tile = pl.program_id(0) * heads
    counts = [count_ref[tile + h] for h in range(heads)]
    most = functools.reduce(jnp.maximum, counts)

    def chunk(h, at, size):
        ks, vs = [], []
        for j in range(size):
            row = list_ref[(tile + h) * slots + at + j] * BLOCK_POSITIONS
            rows = pl.ds(pl.multiple_of(row, BLOCK_POSITIONS), BLOCK_POSITIONS)
            ks.append(key_buf[rows, lanes[h]])
            vs.append(value_buf[rows, lanes[h]])
        query = stacked_heads(q_ref, h * GROUP * HEAD_SIZE)
        scores = dot_t(query, jnp.concatenate(ks, axis=0))
        col = lax.broadcasted_iota(jnp.int32, (1, size * BLOCK_POSITIONS), 1)
        bias = jnp.where(col < (counts[h] - at) * BLOCK_POSITIONS, 0.0, MASKED)
        return scores + bias, jnp.concatenate(vs, axis=0)

    def leading(h, size):
        scores, value_rows = chunk(h, 0, size)
        row = lax.broadcasted_iota(jnp.int32, (scores.shape[0], HEAD_SIZE), 0)
        col = lax.broadcasted_iota(jnp.int32, (scores.shape[0], HEAD_SIZE), 1)
        keep = (col <= row % BLOCK_POSITIONS) | (col >= BLOCK_POSITIONS)
        head_part = jnp.where(keep, scores[:, :HEAD_SIZE], MASKED)
        return jnp.concatenate([head_part, scores[:, HEAD_SIZE:]], axis=1), value_rows

    def give(h, acc, total):
        result = (acc * inverse(total)).astype(out_ref.dtype)
        for g in range(GROUP):
            lane = (h * GROUP + g) * HEAD_SIZE
            rows = slice(g * BLOCK_POSITIONS, (g + 1) * BLOCK_POSITIONS)
            out_ref[:, lane : lane + HEAD_SIZE] = result[rows]

    def put(h, parts):
        working[0][h], working[1][h], working[2][h] = parts

    for low, size in zip((-1,) + LEADS[:-1], LEADS):

        @pl.when((most > low) & (most <= size))
        def _(size=size):
            each_ahead(
                heads,
                lambda h: leading(h, size),
                lambda h, held: give(h, *first_part(*held)[1:]),
            )

    @pl.when(most > LEADS[-1])
    def _():
        each_ahead(
            heads,
            lambda h: leading(h, LEADS[-1]),
            lambda h, held: put(h, first_part(*held)),
        )

        def step(i, carry):
            each_ahead(
                heads,
                lambda h: chunk(h, LEADS[-1] + i * CHUNK, CHUNK),
                lambda h, held: put(h, next_part(*held, *(ref[h] for ref in working))),
            )
            return carry

        lax.fori_loop(0, (most - LEADS[-1] + CHUNK - 1) // CHUNK, step, 0)
        for h in range(heads):
            give(h, working[1][h], working[2][h])


def last_part(queries, packed, counts, scal, dec_query, limit, state, keys, values):
    blocks, heads = queries.shape[0] // BLOCK_POSITIONS, keys[0].shape[1] // HEAD_SIZE
    length, shards = keys[0].shape[0], len(keys)
    slots = packed.shape[0] // (blocks * heads)
    tile_rows = BLOCK_POSITIONS * GROUP
    row_spec = pl.BlockSpec((BLOCK_POSITIONS, queries.shape[1]), lambda b, *_: (b, 0))
    in_hbm = pl.BlockSpec(memory_space=pltpu.HBM)
    dec_spec = pl.BlockSpec(dec_query.shape, lambda b, *_: (0, 0))
    limit_spec = pl.BlockSpec(limit.shape, lambda b, *_: (0, 0))
    return pl.pallas_call(
        functools.partial(last_kernel, shards, heads, slots),
        grid_spec=pltpu.PrefetchScalarGridSpec(
            num_scalar_prefetch=3,
            grid=(blocks,),
            in_specs=[row_spec, dec_spec, limit_spec] + [in_hbm] * (3 + 2 * shards),
            out_specs=[row_spec, dec_spec],
            scratch_shapes=[pltpu.VMEM((shards * length, heads * HEAD_SIZE), keys[0].dtype)] * 2
            + [pltpu.VMEM((heads, tile_rows, HEAD_SIZE), jnp.float32)] * 3
            + [pltpu.VMEM(state[0].shape, jnp.float32)] * 3
            + [pltpu.SemaphoreType.DMA((shards, 2)), pltpu.SemaphoreType.DMA((3,))],
        ),
        out_shape=[
            jax.ShapeDtypeStruct(queries.shape, queries.dtype),
            jax.ShapeDtypeStruct(dec_query.shape, dec_query.dtype),
        ],
        compiler_params=pltpu.CompilerParams(vmem_limit_bytes=VMEM_LIMIT),
        cost_estimate=pl.CostEstimate(flops=1, transcendentals=1, bytes_accessed=1),
        name="prompt",
    )(packed, counts, scal, queries, dec_query, limit, *state, *keys, *values)


def local(
    n, queries, keys, values, block_lists, dec_queries, dec_keys, decode_value_rows, positions
):
    rows = queries.shape[0]
    per_dev = rows // BLOCK_POSITIONS
    half = n // 2
    me = lax.axis_index("seq")

    def ring_place(s):
        return jnp.where(s % 2 == 0, s // 2, n - 1 - s // 2)

    place = ring_place(me)
    forward, backward = ring_orders(n)
    offsets = [0]
    for d in range(1, half):
        offsets += [-d, d]
    offsets += [half]
    at = (place + jnp.array(offsets, jnp.int32)) % n
    starts = jnp.where(at < half, 2 * at, 2 * (n - 1 - at) + 1) * rows

    first = me * per_dev
    mine = lax.dynamic_slice_in_dim(block_lists, first, per_dev, 1).transpose(1, 0, 2)
    valid = mine >= 0
    entry = jnp.maximum(mine, 0)
    delta = (ring_place(entry // per_dev) - place) % n
    slot = jnp.where(delta < half, 2 * delta, 2 * (n - delta) - 1)
    entry = slot * per_dev + entry % per_dev
    slots = -(-entry.shape[-1] // CHUNK) * CHUNK
    packed = jnp.pad(entry, ((0, 0), (0, 0), (0, slots - entry.shape[-1]))).reshape(-1)
    counts = jnp.sum(valid.astype(jnp.int32), axis=-1).reshape(-1)

    owned, steps = dec_queries.shape[0], dec_queries.shape[1]
    limits = lax.dynamic_slice_in_dim(positions, me * owned, owned, 0)
    query = dec_queries.reshape(owned * steps, -1)
    new = (dec_keys.reshape(owned * steps, -1), decode_value_rows.reshape(owned * steps, -1))
    limit = jnp.broadcast_to(
        limits[None, :, None, None], (GROUP, owned, steps, HEAD_SIZE)
    ).reshape(-1, HEAD_SIZE)
    scal = jnp.concatenate([jnp.min(limits)[None], jnp.max(limits)[None], starts])
    decode = functools.partial(decode_part, query, limit, scal)

    shard_keys, shard_values = [keys], [values]
    key_f, value_f, key_b, value_b = keys, values, keys, values
    before = [(), ()]
    for d in range(1, half + 1):
        key_f, key_b, *_ = lax.optimization_barrier((key_f, key_b, *before[0]))
        value_f, value_b, *_ = lax.optimization_barrier((value_f, value_b, *before[1]))
        key_f = lax.ppermute(key_f, "seq", forward)
        value_b = lax.ppermute(value_b, "seq", backward)
        if d < half:
            key_b = lax.ppermute(key_b, "seq", backward)
            value_f = lax.ppermute(value_f, "seq", forward)
            shard_keys += [key_f, key_b]
            shard_values += [value_f, value_b]
        else:
            shard_keys += [key_f]
            shard_values += [value_b]
        before = [(), ()]
        if d == 1:
            state = decode(shard_keys, shard_values, 0, 1, new=new)
            before[1] = (state[0], packed, counts)
        elif d < half:
            state = decode(shard_keys, shard_values, 2 * d - 3, 2 * d - 1, state=state)
            before[1] = (state[0],)
    state = decode(shard_keys, shard_values, n - 3, n - 1, state=state)
    prompt_out, decode_out = last_part(
        queries, packed, counts, scal, query, limit, state, shard_keys, shard_values
    )
    return prompt_out, decode_out.reshape(owned, steps, -1)


def solution(mesh):
    return jax.shard_map(
        functools.partial(local, mesh.shape["seq"]),
        mesh=mesh,
        in_specs=(
            P(("groups", "seq"), "head"),
            P(("groups", "seq"), "head"),
            P(("groups", "seq"), "head"),
            P("head", "groups", None),
            P(("groups", "seq"), None, "head"),
            P(("groups", "seq"), None, "head"),
            P(("groups", "seq"), None, "head"),
            P("groups"),
        ),
        out_specs=(P(("groups", "seq"), "head"), P(("groups", "seq"), None, "head")),
        check_vma=False,
    )
```

```python
import functools
import math

import jax
import jax.numpy as jnp
from jax import lax
from jax.experimental import pallas as pl
from jax.experimental.pallas import tpu as pltpu
from jax.sharding import PartitionSpec as P

QUERY_HEADS = 64
KEY_VALUE_HEADS = 8
HEAD_SIZE = 128
BLOCK_POSITIONS = 64
DECODE_STEPS = 2
GROUP = QUERY_HEADS // KEY_VALUE_HEADS
FACTOR = math.log2(math.e) / math.sqrt(HEAD_SIZE)
MASKED = -1e30
CHUNK = 4
LEADS = (12, 16)
VMEM_LIMIT = 63 * 1024 * 1024


def ring_orders(n):
    ring = list(range(0, n, 2)) + list(range(n - 1, 0, -2))
    forward = [(ring[i], ring[(i + 1) % n]) for i in range(n)]
    return forward, [(b, a) for a, b in forward]


def wide(x, lanes):
    return jnp.concatenate([x] * (lanes // HEAD_SIZE), axis=1) if lanes > HEAD_SIZE else x[:, :lanes]


def dot_t(a, b):
    return lax.dot_general(a, b, (((1,), (1,)), ((), ())), preferred_element_type=jnp.float32)


def first_part(scores, value_rows):
    top = jnp.broadcast_to(jnp.max(scores, axis=1, keepdims=True), (scores.shape[0], HEAD_SIZE))
    weights = jnp.exp2((scores - wide(top, scores.shape[1])) * FACTOR).astype(jnp.bfloat16)
    both = jnp.concatenate([value_rows, jnp.ones_like(value_rows)], axis=1)
    mixed = jnp.dot(weights, both, preferred_element_type=jnp.float32)
    return top, mixed[:, :HEAD_SIZE], mixed[:, HEAD_SIZE:]


def next_part(scores, value_rows, top, acc, total):
    new_top = jnp.maximum(top, jnp.max(scores, axis=1, keepdims=True))
    weights = jnp.exp2((scores - wide(new_top, scores.shape[1])) * FACTOR).astype(jnp.bfloat16)
    shrink = jnp.exp2((top - new_top) * FACTOR)
    both = jnp.concatenate([value_rows, jnp.ones_like(value_rows)], axis=1)
    mixed = jnp.dot(weights, both, preferred_element_type=jnp.float32)
    return new_top, acc * shrink + mixed[:, :HEAD_SIZE], total * shrink + mixed[:, HEAD_SIZE:]


def inverse(x):
    rough = pl.reciprocal(x, approx=True)
    return rough * (2.0 - x * rough)


def each_ahead(count, begin, finish):
    held = begin(0)
    for i in range(count):
        following = begin(i + 1) if i + 1 < count else None
        finish(i, held)
        held = following


def stacked_heads(ref, lane):
    parts = [
        ref[:, lane + g * HEAD_SIZE : lane + (g + 1) * HEAD_SIZE] for g in range(GROUP)
    ]
    return jnp.concatenate(parts, axis=0)


def copy_all(pairs, sem):
    copies = [pltpu.make_async_copy(src, dst, sem.at[i]) for i, (src, dst) in enumerate(pairs)]
    for c in copies:
        c.start()
    return copies


def wait_all(copies):
    for c in copies:
        c.wait()


def decode_kernel(lo, shards, heads, first, *refs):
    refs = list(refs)
    scal = refs.pop(0)
    q_ref, limit_ref = refs.pop(0), refs.pop(0)
    if first:
        nk_ref, nv_ref = refs.pop(0), refs.pop(0)
    else:
        state_in = refs[:3]
        refs = refs[3:]
    keys, values = refs[:shards], refs[shards : 2 * shards]
    refs = refs[2 * shards :]
    state_out = refs[:3]
    refs = refs[3:]
    key_buf, value_buf, top_ref, acc_ref, total_ref, sem, state_sem = refs
    working = (top_ref, acc_ref, total_ref)
    tokens, length = q_ref.shape[0], keys[0].shape[0]
    lanes = [slice(h * HEAD_SIZE, (h + 1) * HEAD_SIZE) for h in range(heads)]
    spans = [pl.ds(i * length, length) for i in range(shards)]
    if not first:
        state_copies = copy_all(zip(state_in, working), state_sem)
    shard_copies = [
        copy_all(
            ((keys[i], key_buf.at[spans[i], :]), (values[i], value_buf.at[spans[i], :])),
            sem.at[i],
        )
        for i in range(shards)
    ]
    query = [stacked_heads(q_ref, h * GROUP * HEAD_SIZE) for h in range(heads)]
    if first:
        def begin(h):
            scores = dot_t(query[h], nk_ref[:, lanes[h]])
            row = lax.broadcasted_iota(jnp.int32, scores.shape, 0) % tokens
            col = lax.broadcasted_iota(jnp.int32, scores.shape, 1)
            allowed = (col <= row) & (col >= row - row % DECODE_STEPS)
            return jnp.where(allowed, scores, MASKED)

        def finish(h, scores):
            top_ref[h], acc_ref[h], total_ref[h] = first_part(scores, nv_ref[:, lanes[h]])

        each_ahead(heads, begin, finish)
    else:
        wait_all(state_copies)
    for i in range(shards):
        wait_all(shard_copies[i])
        start = scal[2 + lo + i]

        def part(masked, i=i, start=start):
            def begin(h):
                scores = dot_t(query[h], key_buf[spans[i], lanes[h]])
                if masked:
                    col = lax.broadcasted_iota(jnp.int32, scores.shape, 1) + start
                    scores = jnp.where(col < wide(limit_ref[...], length), scores, MASKED)
                return scores

            def finish(h, scores):
                top_ref[h], acc_ref[h], total_ref[h] = next_part(
                    scores, value_buf[spans[i], lanes[h]], top_ref[h], acc_ref[h], total_ref[h]
                )

            each_ahead(heads, begin, finish)

        @pl.when(start + length <= scal[0])
        def _():
            part(False)

        @pl.when((start + length > scal[0]) & (start < scal[1]))
        def _():
            part(True)

    wait_all(copy_all(zip(working, state_out), state_sem))


def decode_part(query, limit, scal, keys, values, lo, hi, new=None, state=None):
    keys, values = keys[lo:hi], values[lo:hi]
    tokens, heads = query.shape[0], keys[0].shape[1] // HEAD_SIZE
    rows, length, shards = tokens * GROUP, keys[0].shape[0], hi - lo
    in_vmem = pl.BlockSpec(memory_space=pltpu.VMEM)
    in_hbm = pl.BlockSpec(memory_space=pltpu.HBM)
    state_shape = jax.ShapeDtypeStruct((heads, rows, HEAD_SIZE), jnp.float32)
    more = list(new) if state is None else list(state)
    in_specs = [in_vmem] * 2 + [in_vmem if state is None else in_hbm] * len(more)
    in_specs += [in_hbm] * (2 * shards)
    out_specs, out_shape = [in_hbm] * 3, [state_shape] * 3
    return pl.pallas_call(
        functools.partial(decode_kernel, lo, shards, heads, state is None),
        grid_spec=pltpu.PrefetchScalarGridSpec(
            num_scalar_prefetch=1,
            in_specs=in_specs,
            out_specs=out_specs,
            scratch_shapes=[pltpu.VMEM((shards * length, heads * HEAD_SIZE), keys[0].dtype)] * 2
            + [pltpu.VMEM(state_shape.shape, jnp.float32)] * 3
            + [pltpu.SemaphoreType.DMA((shards, 2)), pltpu.SemaphoreType.DMA((3,))],
        ),
        out_shape=out_shape,
        compiler_params=pltpu.CompilerParams(vmem_limit_bytes=VMEM_LIMIT),
        cost_estimate=pl.CostEstimate(
            flops=1, transcendentals=1, bytes_accessed=1
        ),
        name="decode_first" if state is None else "decode_next",
    )(scal, query, limit, *more, *keys, *values)


def last_kernel(shards, heads, slots, *refs):
    refs = list(refs)
    list_ref, count_ref, scal, q_ref, dec_q_ref, limit_ref = refs[:6]
    state_in = refs[6:9]
    keys, values = refs[9 : 9 + shards], refs[9 + shards : 9 + 2 * shards]
    out_ref, dec_out_ref, key_buf, value_buf = refs[9 + 2 * shards : 13 + 2 * shards]
    working = refs[13 + 2 * shards : 16 + 2 * shards]
    state = refs[16 + 2 * shards : 19 + 2 * shards]
    sem, state_sem = refs[19 + 2 * shards :]
    length = keys[0].shape[0]
    lanes = [slice(h * HEAD_SIZE, (h + 1) * HEAD_SIZE) for h in range(heads)]

    @pl.when(pl.program_id(0) == 0)
    def _():
        state_copies = copy_all(zip(state_in, state), state_sem)
        shard_copies = []
        for i in reversed(range(shards)):
            at = pl.ds(i * length, length)
            pairs = ((keys[i], key_buf.at[at, :]), (values[i], value_buf.at[at, :]))
            shard_copies.append(copy_all(pairs, sem.at[i]))
        tokens = dec_q_ref.shape[0]
        start = scal[2 + shards - 1]
        rows = slice((shards - 1) * length, shards * length)
        wait_all(state_copies)
        wait_all(shard_copies[0])

        def begin(h):
            query = stacked_heads(dec_q_ref, h * GROUP * HEAD_SIZE)
            scores = dot_t(query, key_buf[rows, lanes[h]])
            col = lax.broadcasted_iota(jnp.int32, scores.shape, 1) + start
            return jnp.where(col < wide(limit_ref[...], length), scores, MASKED)

        def finish(h, scores):
            _, acc, total = next_part(
                scores, value_buf[rows, lanes[h]], *(ref[h] for ref in state)
            )
            result = acc * inverse(total)
            for g in range(GROUP):
                lane = (h * GROUP + g) * HEAD_SIZE
                rows_of_g = result[g * tokens : (g + 1) * tokens]
                rows_of_g = rows_of_g.reshape(tokens // DECODE_STEPS, DECODE_STEPS, HEAD_SIZE)
                dec_out_ref[:, :, lane : lane + HEAD_SIZE] = rows_of_g.astype(dec_out_ref.dtype)

        each_ahead(heads, begin, finish)
        for copies in shard_copies[1:]:
            wait_all(copies)

    tile = pl.program_id(0) * heads
    counts = [count_ref[tile + h] for h in range(heads)]
    most = functools.reduce(jnp.maximum, counts)

    def chunk(h, at, size):
        ks, vs = [], []
        for j in range(size):
            row = list_ref[(tile + h) * slots + at + j] * BLOCK_POSITIONS
            rows = pl.ds(pl.multiple_of(row, BLOCK_POSITIONS), BLOCK_POSITIONS)
            ks.append(key_buf[rows, lanes[h]])
            vs.append(value_buf[rows, lanes[h]])
        query = stacked_heads(q_ref, h * GROUP * HEAD_SIZE)
        scores = dot_t(query, jnp.concatenate(ks, axis=0))
        col = lax.broadcasted_iota(jnp.int32, (1, size * BLOCK_POSITIONS), 1)
        bias = jnp.where(col < (counts[h] - at) * BLOCK_POSITIONS, 0.0, MASKED)
        return scores + bias, jnp.concatenate(vs, axis=0)

    def leading(h, size):
        scores, value_rows = chunk(h, 0, size)
        row = lax.broadcasted_iota(jnp.int32, (scores.shape[0], HEAD_SIZE), 0)
        col = lax.broadcasted_iota(jnp.int32, (scores.shape[0], HEAD_SIZE), 1)
        keep = (col <= row % BLOCK_POSITIONS) | (col >= BLOCK_POSITIONS)
        head_part = jnp.where(keep, scores[:, :HEAD_SIZE], MASKED)
        return jnp.concatenate([head_part, scores[:, HEAD_SIZE:]], axis=1), value_rows

    def give(h, acc, total):
        result = (acc * inverse(total)).astype(out_ref.dtype)
        for g in range(GROUP):
            lane = (h * GROUP + g) * HEAD_SIZE
            rows = slice(g * BLOCK_POSITIONS, (g + 1) * BLOCK_POSITIONS)
            out_ref[:, lane : lane + HEAD_SIZE] = result[rows]

    def put(h, parts):
        working[0][h], working[1][h], working[2][h] = parts

    for low, size in zip((-1,) + LEADS[:-1], LEADS):

        @pl.when((most > low) & (most <= size))
        def _(size=size):
            each_ahead(
                heads,
                lambda h: leading(h, size),
                lambda h, held: give(h, *first_part(*held)[1:]),
            )

    @pl.when(most > LEADS[-1])
    def _():
        each_ahead(
            heads,
            lambda h: leading(h, LEADS[-1]),
            lambda h, held: put(h, first_part(*held)),
        )

        def step(i, carry):
            each_ahead(
                heads,
                lambda h: chunk(h, LEADS[-1] + i * CHUNK, CHUNK),
                lambda h, held: put(h, next_part(*held, *(ref[h] for ref in working))),
            )
            return carry

        lax.fori_loop(0, (most - LEADS[-1] + CHUNK - 1) // CHUNK, step, 0)
        for h in range(heads):
            give(h, working[1][h], working[2][h])


def last_part(queries, packed, counts, scal, dec_query, limit, state, keys, values):
    blocks, heads = queries.shape[0] // BLOCK_POSITIONS, keys[0].shape[1] // HEAD_SIZE
    length, shards = keys[0].shape[0], len(keys)
    slots = packed.shape[0] // (blocks * heads)
    tile_rows = BLOCK_POSITIONS * GROUP
    row_spec = pl.BlockSpec((BLOCK_POSITIONS, queries.shape[1]), lambda b, *_: (b, 0))
    in_hbm = pl.BlockSpec(memory_space=pltpu.HBM)
    dec_spec = pl.BlockSpec(dec_query.shape, lambda b, *_: (0, 0))
    dec_shape = (dec_query.shape[0] // DECODE_STEPS, DECODE_STEPS, dec_query.shape[1])
    limit_spec = pl.BlockSpec(limit.shape, lambda b, *_: (0, 0))
    return pl.pallas_call(
        functools.partial(last_kernel, shards, heads, slots),
        grid_spec=pltpu.PrefetchScalarGridSpec(
            num_scalar_prefetch=3,
            grid=(blocks,),
            in_specs=[row_spec, dec_spec, limit_spec] + [in_hbm] * (3 + 2 * shards),
            out_specs=[row_spec, pl.BlockSpec(dec_shape, lambda b, *_: (0, 0, 0))],
            scratch_shapes=[pltpu.VMEM((shards * length, heads * HEAD_SIZE), keys[0].dtype)] * 2
            + [pltpu.VMEM((heads, tile_rows, HEAD_SIZE), jnp.float32)] * 3
            + [pltpu.VMEM(state[0].shape, jnp.float32)] * 3
            + [pltpu.SemaphoreType.DMA((shards, 2)), pltpu.SemaphoreType.DMA((3,))],
        ),
        out_shape=[
            jax.ShapeDtypeStruct(queries.shape, queries.dtype),
            jax.ShapeDtypeStruct(dec_shape, dec_query.dtype),
        ],
        compiler_params=pltpu.CompilerParams(vmem_limit_bytes=VMEM_LIMIT),
        cost_estimate=pl.CostEstimate(flops=1, transcendentals=1, bytes_accessed=1),
        name="prompt",
    )(packed, counts, scal, queries, dec_query, limit, *state, *keys, *values)


def local(
    n, queries, keys, values, block_lists, dec_queries, dec_keys, decode_value_rows, positions
):
    rows = queries.shape[0]
    per_dev = rows // BLOCK_POSITIONS
    half = n // 2
    me = lax.axis_index("seq")

    def ring_place(s):
        return jnp.where(s % 2 == 0, s // 2, n - 1 - s // 2)

    place = ring_place(me)
    forward, backward = ring_orders(n)
    offsets = [0]
    for d in range(1, half):
        offsets += [-d, d]
    offsets += [half]
    at = (place + jnp.array(offsets, jnp.int32)) % n
    starts = jnp.where(at < half, 2 * at, 2 * (n - 1 - at) + 1) * rows

    first = me * per_dev
    mine = lax.dynamic_slice_in_dim(block_lists, first, per_dev, 1).transpose(1, 0, 2)
    valid = mine >= 0
    entry = jnp.maximum(mine, 0)
    delta = (ring_place(entry // per_dev) - place) % n
    slot = jnp.where(delta < half, 2 * delta, 2 * (n - delta) - 1)
    entry = slot * per_dev + entry % per_dev
    slots = -(-entry.shape[-1] // CHUNK) * CHUNK
    packed = jnp.pad(entry, ((0, 0), (0, 0), (0, slots - entry.shape[-1]))).reshape(-1)
    counts = jnp.sum(valid.astype(jnp.int32), axis=-1).reshape(-1)

    owned, steps = dec_queries.shape[0], dec_queries.shape[1]
    limits = lax.dynamic_slice_in_dim(positions, me * owned, owned, 0)
    query = dec_queries.reshape(owned * steps, -1)
    new = (dec_keys.reshape(owned * steps, -1), decode_value_rows.reshape(owned * steps, -1))
    limit = jnp.broadcast_to(
        limits[None, :, None, None], (GROUP, owned, steps, HEAD_SIZE)
    ).reshape(-1, HEAD_SIZE)
    scal = jnp.concatenate([jnp.min(limits)[None], jnp.max(limits)[None], starts])
    decode = functools.partial(decode_part, query, limit, scal)

    shard_keys, shard_values = [keys], [values]
    key_f, value_f, key_b, value_b = keys, values, keys, values
    before = [(), ()]
    for d in range(1, half + 1):
        key_f, key_b, *_ = lax.optimization_barrier((key_f, key_b, *before[0]))
        value_f, value_b, *_ = lax.optimization_barrier((value_f, value_b, *before[1]))
        key_f = lax.ppermute(key_f, "seq", forward)
        value_b = lax.ppermute(value_b, "seq", backward)
        if d < half:
            key_b = lax.ppermute(key_b, "seq", backward)
            value_f = lax.ppermute(value_f, "seq", forward)
            shard_keys += [key_f, key_b]
            shard_values += [value_f, value_b]
        else:
            shard_keys += [key_f]
            shard_values += [value_b]
        before = [(), ()]
        if d == 1:
            state = decode(shard_keys, shard_values, 0, 1, new=new)
            before[1] = (state[0], packed, counts)
        elif d < half:
            state = decode(shard_keys, shard_values, 2 * d - 3, 2 * d - 1, state=state)
            before[1] = (state[0],)
    state = decode(shard_keys, shard_values, n - 3, n - 1, state=state)
    prompt_out, decode_out = last_part(
        queries, packed, counts, scal, query, limit, state, shard_keys, shard_values
    )
    return prompt_out, decode_out


def solution(mesh):
    return jax.shard_map(
        functools.partial(local, mesh.shape["seq"]),
        mesh=mesh,
        in_specs=(
            P(("groups", "seq"), "head"),
            P(("groups", "seq"), "head"),
            P(("groups", "seq"), "head"),
            P("head", "groups", None),
            P(("groups", "seq"), None, "head"),
            P(("groups", "seq"), None, "head"),
            P(("groups", "seq"), None, "head"),
            P("groups"),
        ),
        out_specs=(P(("groups", "seq"), "head"), P(("groups", "seq"), None, "head")),
        check_vma=False,
    )
```

```python
import functools
import math

import jax
import jax.numpy as jnp
from jax import lax
from jax.experimental import pallas as pl
from jax.experimental.pallas import tpu as pltpu
from jax.sharding import PartitionSpec as P

QUERY_HEADS = 64
KEY_VALUE_HEADS = 8
HEAD_SIZE = 128
BLOCK_POSITIONS = 64
DECODE_STEPS = 2
GROUP = QUERY_HEADS // KEY_VALUE_HEADS
FACTOR = math.log2(math.e) / math.sqrt(HEAD_SIZE)
MASKED = -1e30
CHUNK = 4
LEADS = (12,)
VMEM_LIMIT = 63 * 1024 * 1024


def ring_orders(n):
    ring = list(range(0, n, 2)) + list(range(n - 1, 0, -2))
    forward = [(ring[i], ring[(i + 1) % n]) for i in range(n)]
    return forward, [(b, a) for a, b in forward]


def wide(x, lanes):
    return jnp.concatenate([x] * (lanes // HEAD_SIZE), axis=1) if lanes > HEAD_SIZE else x[:, :lanes]


def dot_t(a, b):
    return lax.dot_general(a, b, (((1,), (1,)), ((), ())), preferred_element_type=jnp.float32)


def first_part(scores, value_rows):
    top = jnp.broadcast_to(jnp.max(scores, axis=1, keepdims=True), (scores.shape[0], HEAD_SIZE))
    weights = jnp.exp2((scores - wide(top, scores.shape[1])) * FACTOR).astype(jnp.bfloat16)
    both = jnp.concatenate([value_rows, jnp.ones_like(value_rows)], axis=1)
    mixed = jnp.dot(weights, both, preferred_element_type=jnp.float32)
    return top, mixed[:, :HEAD_SIZE], mixed[:, HEAD_SIZE:]


def next_part(scores, value_rows, top, acc, total):
    new_top = jnp.maximum(top, jnp.max(scores, axis=1, keepdims=True))
    weights = jnp.exp2((scores - wide(new_top, scores.shape[1])) * FACTOR).astype(jnp.bfloat16)
    shrink = jnp.exp2((top - new_top) * FACTOR)
    both = jnp.concatenate([value_rows, jnp.ones_like(value_rows)], axis=1)
    mixed = jnp.dot(weights, both, preferred_element_type=jnp.float32)
    return new_top, acc * shrink + mixed[:, :HEAD_SIZE], total * shrink + mixed[:, HEAD_SIZE:]


def inverse(x):
    rough = pl.reciprocal(x, approx=True)
    return rough * (2.0 - x * rough)


def each_ahead(count, begin, finish):
    held = begin(0)
    for i in range(count):
        following = begin(i + 1) if i + 1 < count else None
        finish(i, held)
        held = following


def stacked_heads(ref, lane):
    parts = [
        ref[:, lane + g * HEAD_SIZE : lane + (g + 1) * HEAD_SIZE] for g in range(GROUP)
    ]
    return jnp.concatenate(parts, axis=0)


def copy_all(pairs, sem):
    copies = [pltpu.make_async_copy(src, dst, sem.at[i]) for i, (src, dst) in enumerate(pairs)]
    for c in copies:
        c.start()
    return copies


def wait_all(copies):
    for c in copies:
        c.wait()


def decode_kernel(lo, shards, heads, first, *refs):
    refs = list(refs)
    scal = refs.pop(0)
    q_ref, limit_ref = refs.pop(0), refs.pop(0)
    if first:
        nk_ref, nv_ref = refs.pop(0), refs.pop(0)
    else:
        state_in = refs[:3]
        refs = refs[3:]
    keys, values = refs[:shards], refs[shards : 2 * shards]
    refs = refs[2 * shards :]
    state_out = refs[:3]
    refs = refs[3:]
    key_buf, value_buf, top_ref, acc_ref, total_ref, sem, state_sem = refs
    working = (top_ref, acc_ref, total_ref)
    tokens, length = q_ref.shape[0], keys[0].shape[0]
    lanes = [slice(h * HEAD_SIZE, (h + 1) * HEAD_SIZE) for h in range(heads)]
    spans = [pl.ds(i * length, length) for i in range(shards)]
    if not first:
        state_copies = copy_all(zip(state_in, working), state_sem)
    shard_copies = [
        copy_all(
            ((keys[i], key_buf.at[spans[i], :]), (values[i], value_buf.at[spans[i], :])),
            sem.at[i],
        )
        for i in range(shards)
    ]
    query = [stacked_heads(q_ref, h * GROUP * HEAD_SIZE) for h in range(heads)]
    if first:
        def begin(h):
            scores = dot_t(query[h], nk_ref[:, lanes[h]])
            row = lax.broadcasted_iota(jnp.int32, scores.shape, 0) % tokens
            col = lax.broadcasted_iota(jnp.int32, scores.shape, 1)
            allowed = (col <= row) & (col >= row - row % DECODE_STEPS)
            return jnp.where(allowed, scores, MASKED)

        def finish(h, scores):
            top_ref[h], acc_ref[h], total_ref[h] = first_part(scores, nv_ref[:, lanes[h]])

        each_ahead(heads, begin, finish)
    else:
        wait_all(state_copies)
    for i in range(shards):
        wait_all(shard_copies[i])
        start = scal[2 + lo + i]

        def part(masked, i=i, start=start):
            def begin(h):
                scores = dot_t(query[h], key_buf[spans[i], lanes[h]])
                if masked:
                    col = lax.broadcasted_iota(jnp.int32, scores.shape, 1) + start
                    scores = jnp.where(col < wide(limit_ref[...], length), scores, MASKED)
                return scores

            def finish(h, scores):
                top_ref[h], acc_ref[h], total_ref[h] = next_part(
                    scores, value_buf[spans[i], lanes[h]], top_ref[h], acc_ref[h], total_ref[h]
                )

            each_ahead(heads, begin, finish)

        @pl.when(start + length <= scal[0])
        def _():
            part(False)

        @pl.when((start + length > scal[0]) & (start < scal[1]))
        def _():
            part(True)

    wait_all(copy_all(zip(working, state_out), state_sem))


def decode_part(query, limit, scal, keys, values, lo, hi, new=None, state=None):
    keys, values = keys[lo:hi], values[lo:hi]
    tokens, heads = query.shape[0], keys[0].shape[1] // HEAD_SIZE
    rows, length, shards = tokens * GROUP, keys[0].shape[0], hi - lo
    in_vmem = pl.BlockSpec(memory_space=pltpu.VMEM)
    in_hbm = pl.BlockSpec(memory_space=pltpu.HBM)
    state_shape = jax.ShapeDtypeStruct((heads, rows, HEAD_SIZE), jnp.float32)
    more = list(new) if state is None else list(state)
    in_specs = [in_vmem] * 2 + [in_vmem if state is None else in_hbm] * len(more)
    in_specs += [in_hbm] * (2 * shards)
    out_specs, out_shape = [in_hbm] * 3, [state_shape] * 3
    return pl.pallas_call(
        functools.partial(decode_kernel, lo, shards, heads, state is None),
        grid_spec=pltpu.PrefetchScalarGridSpec(
            num_scalar_prefetch=1,
            in_specs=in_specs,
            out_specs=out_specs,
            scratch_shapes=[pltpu.VMEM((shards * length, heads * HEAD_SIZE), keys[0].dtype)] * 2
            + [pltpu.VMEM(state_shape.shape, jnp.float32)] * 3
            + [pltpu.SemaphoreType.DMA((shards, 2)), pltpu.SemaphoreType.DMA((3,))],
        ),
        out_shape=out_shape,
        compiler_params=pltpu.CompilerParams(vmem_limit_bytes=VMEM_LIMIT),
        cost_estimate=pl.CostEstimate(
            flops=1, transcendentals=1, bytes_accessed=1
        ),
        name="decode_first" if state is None else "decode_next",
    )(scal, query, limit, *more, *keys, *values)


def last_kernel(shards, heads, slots, *refs):
    refs = list(refs)
    list_ref, count_ref, scal, q_ref, dec_q_ref, limit_ref = refs[:6]
    state_in = refs[6:9]
    keys, values = refs[9 : 9 + shards], refs[9 + shards : 9 + 2 * shards]
    out_ref, dec_out_ref, key_buf, value_buf = refs[9 + 2 * shards : 13 + 2 * shards]
    working = refs[13 + 2 * shards : 16 + 2 * shards]
    state = refs[16 + 2 * shards : 19 + 2 * shards]
    sem, state_sem = refs[19 + 2 * shards :]
    length = keys[0].shape[0]
    lanes = [slice(h * HEAD_SIZE, (h + 1) * HEAD_SIZE) for h in range(heads)]

    @pl.when(pl.program_id(0) == 0)
    def _():
        state_copies = copy_all(zip(state_in, state), state_sem)
        shard_copies = []
        for i in reversed(range(shards)):
            at = pl.ds(i * length, length)
            pairs = ((keys[i], key_buf.at[at, :]), (values[i], value_buf.at[at, :]))
            shard_copies.append(copy_all(pairs, sem.at[i]))
        tokens = dec_q_ref.shape[0]
        start = scal[2 + shards - 1]
        rows = slice((shards - 1) * length, shards * length)
        wait_all(state_copies)
        wait_all(shard_copies[0])

        def begin(h):
            query = stacked_heads(dec_q_ref, h * GROUP * HEAD_SIZE)
            scores = dot_t(query, key_buf[rows, lanes[h]])
            col = lax.broadcasted_iota(jnp.int32, scores.shape, 1) + start
            return jnp.where(col < wide(limit_ref[...], length), scores, MASKED)

        def finish(h, scores):
            _, acc, total = next_part(
                scores, value_buf[rows, lanes[h]], *(ref[h] for ref in state)
            )
            result = acc * inverse(total)
            for g in range(GROUP):
                lane = (h * GROUP + g) * HEAD_SIZE
                rows_of_g = result[g * tokens : (g + 1) * tokens]
                rows_of_g = rows_of_g.reshape(tokens // DECODE_STEPS, DECODE_STEPS, HEAD_SIZE)
                dec_out_ref[:, :, lane : lane + HEAD_SIZE] = rows_of_g.astype(dec_out_ref.dtype)

        each_ahead(heads, begin, finish)
        for copies in shard_copies[1:]:
            wait_all(copies)

    tile = pl.program_id(0) * heads
    counts = [count_ref[tile + h] for h in range(heads)]
    most = functools.reduce(jnp.maximum, counts)

    def chunk(h, at, size):
        ks, vs = [], []
        for j in range(size):
            row = list_ref[(tile + h) * slots + at + j] * BLOCK_POSITIONS
            rows = pl.ds(pl.multiple_of(row, BLOCK_POSITIONS), BLOCK_POSITIONS)
            ks.append(key_buf[rows, lanes[h]])
            vs.append(value_buf[rows, lanes[h]])
        query = stacked_heads(q_ref, h * GROUP * HEAD_SIZE)
        scores = dot_t(query, jnp.concatenate(ks, axis=0))
        col = lax.broadcasted_iota(jnp.int32, (1, size * BLOCK_POSITIONS), 1)
        bias = jnp.where(col < (counts[h] - at) * BLOCK_POSITIONS, 0.0, MASKED)
        return scores + bias, jnp.concatenate(vs, axis=0)

    def leading(h, size):
        scores, value_rows = chunk(h, 0, size)
        row = lax.broadcasted_iota(jnp.int32, (scores.shape[0], HEAD_SIZE), 0)
        col = lax.broadcasted_iota(jnp.int32, (scores.shape[0], HEAD_SIZE), 1)
        keep = (col <= row % BLOCK_POSITIONS) | (col >= BLOCK_POSITIONS)
        head_part = jnp.where(keep, scores[:, :HEAD_SIZE], MASKED)
        return jnp.concatenate([head_part, scores[:, HEAD_SIZE:]], axis=1), value_rows

    def give(h, acc, total):
        result = (acc * inverse(total)).astype(out_ref.dtype)
        for g in range(GROUP):
            lane = (h * GROUP + g) * HEAD_SIZE
            rows = slice(g * BLOCK_POSITIONS, (g + 1) * BLOCK_POSITIONS)
            out_ref[:, lane : lane + HEAD_SIZE] = result[rows]

    def put(h, parts):
        working[0][h], working[1][h], working[2][h] = parts

    for low, size in zip((-1,) + LEADS[:-1], LEADS):

        @pl.when((most > low) & (most <= size))
        def _(size=size):
            each_ahead(
                heads,
                lambda h: leading(h, size),
                lambda h, held: give(h, *first_part(*held)[1:]),
            )

    @pl.when(most > LEADS[-1])
    def _():
        each_ahead(
            heads,
            lambda h: leading(h, LEADS[-1]),
            lambda h, held: put(h, first_part(*held)),
        )

        def step(i, carry):
            each_ahead(
                heads,
                lambda h: chunk(h, LEADS[-1] + i * CHUNK, CHUNK),
                lambda h, held: put(h, next_part(*held, *(ref[h] for ref in working))),
            )
            return carry

        lax.fori_loop(0, (most - LEADS[-1] + CHUNK - 1) // CHUNK, step, 0)
        for h in range(heads):
            give(h, working[1][h], working[2][h])


def last_part(queries, packed, counts, scal, dec_query, limit, state, keys, values):
    blocks, heads = queries.shape[0] // BLOCK_POSITIONS, keys[0].shape[1] // HEAD_SIZE
    length, shards = keys[0].shape[0], len(keys)
    slots = packed.shape[0] // (blocks * heads)
    tile_rows = BLOCK_POSITIONS * GROUP
    row_spec = pl.BlockSpec((BLOCK_POSITIONS, queries.shape[1]), lambda b, *_: (b, 0))
    in_hbm = pl.BlockSpec(memory_space=pltpu.HBM)
    dec_spec = pl.BlockSpec(dec_query.shape, lambda b, *_: (0, 0))
    dec_shape = (dec_query.shape[0] // DECODE_STEPS, DECODE_STEPS, dec_query.shape[1])
    limit_spec = pl.BlockSpec(limit.shape, lambda b, *_: (0, 0))
    return pl.pallas_call(
        functools.partial(last_kernel, shards, heads, slots),
        grid_spec=pltpu.PrefetchScalarGridSpec(
            num_scalar_prefetch=3,
            grid=(blocks,),
            in_specs=[row_spec, dec_spec, limit_spec] + [in_hbm] * (3 + 2 * shards),
            out_specs=[row_spec, pl.BlockSpec(dec_shape, lambda b, *_: (0, 0, 0))],
            scratch_shapes=[pltpu.VMEM((shards * length, heads * HEAD_SIZE), keys[0].dtype)] * 2
            + [pltpu.VMEM((heads, tile_rows, HEAD_SIZE), jnp.float32)] * 3
            + [pltpu.VMEM(state[0].shape, jnp.float32)] * 3
            + [pltpu.SemaphoreType.DMA((shards, 2)), pltpu.SemaphoreType.DMA((3,))],
        ),
        out_shape=[
            jax.ShapeDtypeStruct(queries.shape, queries.dtype),
            jax.ShapeDtypeStruct(dec_shape, dec_query.dtype),
        ],
        compiler_params=pltpu.CompilerParams(vmem_limit_bytes=VMEM_LIMIT),
        cost_estimate=pl.CostEstimate(flops=1, transcendentals=1, bytes_accessed=1),
        name="prompt",
    )(packed, counts, scal, queries, dec_query, limit, *state, *keys, *values)


def local(
    n, queries, keys, values, block_lists, dec_queries, dec_keys, decode_value_rows, positions
):
    rows = queries.shape[0]
    per_dev = rows // BLOCK_POSITIONS
    half = n // 2
    me = lax.axis_index("seq")

    def ring_place(s):
        return jnp.where(s % 2 == 0, s // 2, n - 1 - s // 2)

    place = ring_place(me)
    forward, backward = ring_orders(n)
    offsets = [0]
    for d in range(1, half):
        offsets += [-d, d]
    offsets += [half]
    at = (place + jnp.array(offsets, jnp.int32)) % n
    starts = jnp.where(at < half, 2 * at, 2 * (n - 1 - at) + 1) * rows

    first = me * per_dev
    mine = lax.dynamic_slice_in_dim(block_lists, first, per_dev, 1).transpose(1, 0, 2)
    valid = mine >= 0
    entry = jnp.maximum(mine, 0)
    delta = (ring_place(entry // per_dev) - place) % n
    slot = jnp.where(delta < half, 2 * delta, 2 * (n - delta) - 1)
    entry = slot * per_dev + entry % per_dev
    slots = -(-entry.shape[-1] // CHUNK) * CHUNK
    packed = jnp.pad(entry, ((0, 0), (0, 0), (0, slots - entry.shape[-1]))).reshape(-1)
    counts = jnp.sum(valid.astype(jnp.int32), axis=-1).reshape(-1)

    owned, steps = dec_queries.shape[0], dec_queries.shape[1]
    limits = lax.dynamic_slice_in_dim(positions, me * owned, owned, 0)
    query = dec_queries.reshape(owned * steps, -1)
    new = (dec_keys.reshape(owned * steps, -1), decode_value_rows.reshape(owned * steps, -1))
    limit = jnp.broadcast_to(
        limits[None, :, None, None], (GROUP, owned, steps, HEAD_SIZE)
    ).reshape(-1, HEAD_SIZE)
    scal = jnp.concatenate([jnp.min(limits)[None], jnp.max(limits)[None], starts])
    decode = functools.partial(decode_part, query, limit, scal)

    shard_keys, shard_values = [keys], [values]
    key_f, value_f, key_b, value_b = keys, values, keys, values
    before = [(), ()]
    for d in range(1, half + 1):
        key_f, key_b, *_ = lax.optimization_barrier((key_f, key_b, *before[0]))
        value_f, value_b, *_ = lax.optimization_barrier((value_f, value_b, *before[1]))
        key_f = lax.ppermute(key_f, "seq", forward)
        value_b = lax.ppermute(value_b, "seq", backward)
        if d < half:
            key_b = lax.ppermute(key_b, "seq", backward)
            value_f = lax.ppermute(value_f, "seq", forward)
            shard_keys += [key_f, key_b]
            shard_values += [value_f, value_b]
        else:
            shard_keys += [key_f]
            shard_values += [value_b]
        before = [(), ()]
        if d == 1:
            state = decode(shard_keys, shard_values, 0, 1, new=new)
            before[1] = (state[0], packed, counts)
        elif d < half:
            state = decode(shard_keys, shard_values, 2 * d - 3, 2 * d - 1, state=state)
            before[1] = (state[0],)
    state = decode(shard_keys, shard_values, n - 3, n - 1, state=state)
    prompt_out, decode_out = last_part(
        queries, packed, counts, scal, query, limit, state, shard_keys, shard_values
    )
    return prompt_out, decode_out


def solution(mesh):
    return jax.shard_map(
        functools.partial(local, mesh.shape["seq"]),
        mesh=mesh,
        in_specs=(
            P(("groups", "seq"), "head"),
            P(("groups", "seq"), "head"),
            P(("groups", "seq"), "head"),
            P("head", "groups", None),
            P(("groups", "seq"), None, "head"),
            P(("groups", "seq"), None, "head"),
            P(("groups", "seq"), None, "head"),
            P("groups"),
        ),
        out_specs=(P(("groups", "seq"), "head"), P(("groups", "seq"), None, "head")),
        check_vma=False,
    )
```
